128 devices in a mesh: lat: 8 (over x, y_hi), lon: 16 (over z, y_lo, core).
Axes of the slice: x: 4, y: 4 (y_hi: 2, y_lo: 2; y = y_hi * 2 + y_lo), z: 4, core: 2. Of those that a mesh axis runs over, the one named last changes fastest.
Arguments:
- stash_input: int32 [48, 32, 7200], P(None, 'lat', 'lon'), may hold values from 0 to 255
- input_low: bfloat16 [3, 32, 7200], P(None, 'lat', 'lon'), as said below
- input_high: bfloat16 [3, 32, 7200], P(None, 'lat', 'lon'), as said below
- stash_hidden: int32 [192, 32, 7200], P(None, 'lat', 'lon'), may hold values from 0 to 255
- hidden_low: bfloat16 [12, 32, 7200], P(None, 'lat', 'lon'), as said below
- hidden_high: bfloat16 [12, 32, 7200], P(None, 'lat', 'lon'), as said below
- grad_out: bfloat16 [192, 32, 7200], P(None, 'lat', 'lon'), may hold values from -6 to 6
- kernel: float32 [192, 7, 7], replicated, may hold values from -0.875 to 0.875
- conv_bias: float32 [192], replicated, may hold values from -3 to 3
- norm_gain: float32 [192], replicated, may hold values from 0.25 to 1.75
- norm_bias: float32 [192], replicated, may hold values from -3 to 3
- w_in: bfloat16 [192, 768], replicated, may hold values from -0.4375 to 0.4375
- w_out: bfloat16 [768, 192], replicated, may hold values from -0.21875 to 0.21875
- out_bias: float32 [192], replicated, may hold values from -4 to 4
- layer_scale: float32 [192], replicated, may hold values from 0.5 to 1.5
Outputs:
- grad_input: bfloat16 [192, 32, 7200], P(None, 'lat', 'lon')
- grad_kernel: float32 [192, 7, 7], replicated
- grad_conv_bias: float32 [192], replicated
- grad_norm_gain: float32 [192], replicated
- grad_norm_bias: float32 [192], replicated
- grad_w_in: float32 [192, 768], replicated
- grad_w_out: float32 [768, 192], replicated
- grad_out_bias: float32 [192], replicated
- grad_layer_scale: float32 [192], replicated
The draws below stay inside these ranges and needn't reach their ends.
Inputs may be any that keep to these rules, and one draw needn't show every extreme that they name: `stash_input`: each word packs four 2-bit codes in its low eight bits. `stash_hidden`: each word packs four 2-bit codes in its low eight bits. `input_low`: below input_high at every entry. `input_high`: above input_low at every entry. `hidden_low`: below hidden_high at every entry. `hidden_high`: above hidden_low at every entry.
All inputs are finite; a program needn't handle non-finite values.
Results may differ from the reference program's by a relative error of at most 0.008.
Values may be sent and summed in bfloat16 or wider, within the bound.
No kernel may reach another device: no remote copies, remote signals or barrier semaphores. Data moves between devices by JAX's collectives and lax.ppermute only.
A program may use at most 128 MiB of HBM per device.

```python
import math
import jax
import jax.numpy as jnp
from jax import lax

C = 192
FF = 768
GROUP = 64
RADIUS = 3
RDEV = 4
NH = 32
NW = 7200


def stash_bounds(key, groups, spread_lo, spread_hi):
    grid_shape = (groups, NH, NW)
    center = jax.random.normal(jax.random.fold_in(key, 1), grid_shape, jnp.float32)
    spread = jnp.exp(jax.random.uniform(jax.random.fold_in(key, 2), grid_shape, jnp.float32, math.log(spread_lo), math.log(spread_hi)))
    return (center - 0.5 * spread, center + 0.5 * spread)


def draw_input_low(key, part):
    bounds = stash_bounds(jax.random.fold_in(key, 11), C // GROUP, 0.3, 3.0)
    return bounds[0].astype(jnp.bfloat16)


def draw_input_high(key, part):
    bounds = stash_bounds(jax.random.fold_in(key, 11), C // GROUP, 0.3, 3.0)
    return bounds[1].astype(jnp.bfloat16)


def draw_hidden_low(key, part):
    bounds = stash_bounds(jax.random.fold_in(key, 12), FF // GROUP, 0.3, 3.0)
    return bounds[0].astype(jnp.bfloat16)


def draw_hidden_high(key, part):
    bounds = stash_bounds(jax.random.fold_in(key, 12), FF // GROUP, 0.3, 3.0)
    return bounds[1].astype(jnp.bfloat16)


def plant(values, own_key, smallest, top_value):
    dims = values.shape
    spot = [jax.random.randint(jax.random.fold_in(own_key, axis), (), 0, dims[axis]) for axis in range(len(dims))]
    values = values.at[tuple(spot)].set(smallest)
    longest = dims.index(max(dims))
    spot[longest] = (spot[longest] + 1) % dims[longest]
    return values.at[tuple(spot)].set(top_value)


def steps_of(own_key, dims, shards, smallest, largest):
    def one(dim, blocks):
        steps = jax.random.uniform(jax.random.fold_in(jax.random.fold_in(own_key, 6), dim), (blocks,), jnp.float32, smallest / len(shards), largest / len(shards))
        return jnp.repeat(jnp.exp(steps), dims[dim] // blocks).reshape((-1,) + (1,) * (len(dims) - dim - 1))

    level = one(*shards[0])
    for cut in shards[1:]:
        level = level * one(*cut)
    return level


def bell_draw(stream_key, dims, deviation, most, cuts=(), kind=jnp.bfloat16):
    values = deviation * jax.random.normal(stream_key, dims, jnp.float32)
    if cuts:
        values = values * steps_of(stream_key, dims, cuts, -0.22, 0.18)
    return jnp.clip(values, -most, most).astype(kind)


def setup_inputs(seed: int = 0) -> dict:
    streams_of = jax.random.split(jax.random.key(seed), 16)
    return {
        "stash_input": plant(jax.random.randint(streams_of[0], (C // 4, NH, NW), 0, 256), jax.random.fold_in(streams_of[0], 1), 0, 255).astype(jnp.int32),
        "input_low": draw_input_low(jax.random.fold_in(streams_of[15], 71), 0),
        "input_high": draw_input_high(jax.random.fold_in(streams_of[15], 71), 0),
        "stash_hidden": plant(jax.random.randint(streams_of[3], (FF // 4, NH, NW), 0, 256), jax.random.fold_in(streams_of[3], 1), 0, 255).astype(jnp.int32),
        "hidden_low": draw_hidden_low(jax.random.fold_in(streams_of[15], 71), 0),
        "hidden_high": draw_hidden_high(jax.random.fold_in(streams_of[15], 71), 0),
        "grad_out": bell_draw(streams_of[6], (C, NH, NW), 1.0, 6.0, ((1, 8), (2, 16))),
        "kernel": bell_draw(streams_of[7], (C, 2 * RADIUS + 1, 2 * RADIUS + 1), ((2 * RADIUS + 1) ** 2) ** -0.5, 0.875, (), jnp.float32),
        "conv_bias": bell_draw(streams_of[8], (C,), 0.5, 3.0, (), jnp.float32),
        "norm_gain": jnp.clip(1.0 + 0.15 * jax.random.normal(streams_of[9], (C,), jnp.float32), 0.25, 1.75),
        "norm_bias": bell_draw(streams_of[10], (C,), 0.5, 3.0, (), jnp.float32),
        "w_in": bell_draw(streams_of[11], (C, FF), C ** -0.5, 0.4375),
        "w_out": bell_draw(streams_of[12], (FF, C), FF ** -0.5, 0.21875),
        "out_bias": bell_draw(streams_of[13], (C,), 1.0, 4.0, (), jnp.float32),
        "layer_scale": jnp.clip(jax.random.uniform(streams_of[14], (C,), jnp.float32, 0.5, 1.5), 0.5, 1.5),
    }


def restore(packed, lowest, highest):
    pieces = [jnp.bitwise_and(jnp.right_shift(packed, 2 * bit_pair), 3) for bit_pair in range(4)]
    symbols = jnp.stack(pieces, axis=1).reshape((packed.shape[0] * 4,) + packed.shape[1:]).astype(jnp.float32)
    bottom = jnp.repeat(lowest.astype(jnp.float32), GROUP, axis=0)
    summit = jnp.repeat(highest.astype(jnp.float32), GROUP, axis=0)
    return bottom + symbols * (summit - bottom) / 3.0

def pad_grid(field):
    wrapped = jnp.concatenate([field[:, :, -RADIUS:], field, field[:, :, :RADIUS]], axis=2)
    return jnp.pad(wrapped, ((0, 0), (RADIUS, RADIUS), (0, 0)))

def forward_taps(padded, kernel, rows, cols):
    total = jnp.zeros((padded.shape[0], rows, cols), jnp.float32)
    for row_tap in range(2 * RADIUS + 1):
        for col_tap in range(2 * RADIUS + 1):
            total = total + kernel[:, row_tap, col_tap][:, None, None] * padded[:, row_tap:row_tap + rows, col_tap:col_tap + cols]
    return total

def backward_taps(padded, kernel, rows, cols):
    total = jnp.zeros((padded.shape[0], rows, cols), jnp.float32)
    for row_tap in range(2 * RADIUS + 1):
        for col_tap in range(2 * RADIUS + 1):
            row_start = 2 * RADIUS - row_tap
            col_start = 2 * RADIUS - col_tap
            total = total + kernel[:, row_tap, col_tap][:, None, None] * padded[:, row_start:row_start + rows, col_start:col_start + cols]
    return total

def tap_products(grad_field, padded, rows, cols):
    outer = []
    for row_tap in range(2 * RADIUS + 1):
        inner = [lax.optimization_barrier(jnp.sum(grad_field * padded[:, row_tap:row_tap + rows, col_tap:col_tap + cols], axis=(1, 2))) for col_tap in range(2 * RADIUS + 1)]
        outer.append(jnp.stack(inner, axis=1))
    return jnp.stack(outer, axis=1)

def block_backward(conv_out, hidden_pre, grad_block, norm_gain, norm_bias, w_in, w_out, out_bias, layer_scale):
    channels, rows, cols = conv_out.shape
    count = rows * cols
    flat_conv = conv_out.reshape(channels, count)
    mean_val = lax.optimization_barrier(jnp.mean(flat_conv, axis=0))
    centered = flat_conv - mean_val
    variance = lax.optimization_barrier(jnp.mean(centered * centered, axis=0))
    inv_std = lax.rsqrt(variance + 1e-06)
    normed = centered * inv_std
    normed_in = (normed * norm_gain[:, None] + norm_bias[:, None]).astype(jnp.bfloat16)
    hidden = hidden_pre.reshape(hidden_pre.shape[0], count)
    cdf = 0.5 * (1.0 + jax.scipy.special.erf(hidden * 0.7071067811865476))
    density = jnp.exp(-0.5 * hidden * hidden) * 0.3989422804014327
    active = (hidden * cdf).astype(jnp.bfloat16)
    grad_flat = grad_block.reshape(channels, count).astype(jnp.float32)
    scaled = layer_scale[:, None] * grad_flat
    scaled_in = scaled.astype(jnp.bfloat16)
    contract_cells = (((1,), (1,)), ((), ()))
    grad_w_out = lax.dot_general(active, scaled_in, contract_cells, preferred_element_type=jnp.float32)
    grad_active = jnp.dot(w_out, scaled_in, preferred_element_type=jnp.float32)
    grad_hidden = (grad_active * (cdf + hidden * density)).astype(jnp.bfloat16)
    grad_w_in = lax.dot_general(normed_in, grad_hidden, contract_cells, preferred_element_type=jnp.float32)
    grad_normed = jnp.dot(w_in, grad_hidden, preferred_element_type=jnp.float32)
    recomputed = lax.dot_general(w_out, active, (((0,), (0,)), ((), ())), preferred_element_type=jnp.float32) + out_bias[:, None]
    grad_scale = lax.optimization_barrier(jnp.sum(grad_flat * recomputed, axis=1))
    grad_obias = lax.optimization_barrier(jnp.sum(scaled, axis=1))
    grad_gain = lax.optimization_barrier(jnp.sum(grad_normed * normed, axis=1))
    grad_nbias = lax.optimization_barrier(jnp.sum(grad_normed, axis=1))
    grad_dn = grad_normed * norm_gain[:, None]
    grad_conv = inv_std * (grad_dn - lax.optimization_barrier(jnp.mean(grad_dn, axis=0)) - normed * lax.optimization_barrier(jnp.mean(grad_dn * normed, axis=0)))
    grad_conv = grad_conv.astype(jnp.bfloat16).reshape(channels, rows, cols)
    return (grad_conv, (grad_w_in, grad_w_out, grad_obias, grad_scale, grad_gain, grad_nbias))

def reference(stash_input, input_low, input_high, stash_hidden, hidden_low, hidden_high, grad_out, kernel, conv_bias, norm_gain, norm_bias, w_in, w_out, out_bias, layer_scale):
    block_rows = RDEV
    blocks = NH // block_rows
    restored = restore(stash_input, input_low, input_high).astype(jnp.bfloat16)
    padded_in = pad_grid(restored)

    def first_pass(carry, index):
        start = (index * block_rows).astype(jnp.int32)
        window = lax.dynamic_slice_in_dim(padded_in, start, block_rows + 2 * RADIUS, 1).astype(jnp.float32)
        conv_out = forward_taps(window, kernel, block_rows, NW) + conv_bias[:, None, None]
        hidden_pre = restore(lax.dynamic_slice_in_dim(stash_hidden, start, block_rows, 1), lax.dynamic_slice_in_dim(hidden_low, start, block_rows, 1), lax.dynamic_slice_in_dim(hidden_high, start, block_rows, 1))
        grad_block = lax.dynamic_slice_in_dim(grad_out, start, block_rows, 1)
        grad_conv, parts = block_backward(conv_out, hidden_pre, grad_block, norm_gain, norm_bias, w_in, w_out, out_bias, layer_scale)
        return (tuple((total + part for total, part in zip(carry, parts))), grad_conv)
    zero_c = jnp.zeros((C,), jnp.float32)
    start_sums = (jnp.zeros((C, FF), jnp.float32), jnp.zeros((FF, C), jnp.float32), zero_c, zero_c, zero_c, zero_c)
    mlp_sums, conv_blocks = lax.scan(first_pass, start_sums, jnp.arange(blocks, dtype=jnp.int32))
    grad_conv = jnp.transpose(conv_blocks, (1, 0, 2, 3)).reshape(C, NH, NW)
    padded_grad = pad_grid(grad_conv)

    def second_pass(carry, index):
        start = (index * block_rows).astype(jnp.int32)
        grad_window = lax.dynamic_slice_in_dim(padded_grad, start, block_rows + 2 * RADIUS, 1).astype(jnp.float32)
        in_window = lax.dynamic_slice_in_dim(padded_in, start, block_rows + 2 * RADIUS, 1).astype(jnp.float32)
        grad_block = lax.dynamic_slice_in_dim(grad_out, start, block_rows, 1).astype(jnp.float32)
        own_grad = grad_window[:, RADIUS:RADIUS + block_rows, RADIUS:RADIUS + NW]
        result = (grad_block + backward_taps(grad_window, kernel, block_rows, NW)).astype(jnp.bfloat16)
        kernel_part = tap_products(own_grad, in_window, block_rows, NW)
        return ((carry[0] + kernel_part, carry[1] + lax.optimization_barrier(jnp.sum(own_grad, axis=(1, 2)))), result)
    taps = 2 * RADIUS + 1
    stencil_sums, input_blocks = lax.scan(second_pass, (jnp.zeros((C, taps, taps), jnp.float32), zero_c), jnp.arange(blocks, dtype=jnp.int32))
    grad_input = jnp.transpose(input_blocks, (1, 0, 2, 3)).reshape(C, NH, NW)
    factor = 1.0 / math.sqrt(NH * NW)
    grad_w_in, grad_w_out, grad_obias, grad_scale, grad_gain, grad_nbias = mlp_sums
    return (grad_input, stencil_sums[0] * factor, stencil_sums[1] * factor, grad_gain * factor, grad_nbias * factor, grad_w_in * factor, grad_w_out * factor, grad_obias * factor, grad_scale * factor)
```

```python
import functools
import math

import jax
import jax.numpy as jnp
from jax import lax
from jax.experimental import pallas as pl
from jax.experimental.pallas import tpu as pltpu
from jax.sharding import PartitionSpec as P

C = 192
FF = 768
WORDS = FF // 4
GROUP = 64
RADIUS = 3
TAPS = 2 * RADIUS + 1
ROWS = 4
COLS = 450
WIDE = COLS + 2 * RADIUS
LANES = 512
MAIN = 384
TAIL = COLS + RADIUS - MAIN
PACK = 1408
RIM = MAIN * RADIUS + TAIL * RADIUS - (PACK - 128)
CH = 16
TIE = 3
F32 = jnp.float32
BF16 = jnp.bfloat16
VMEM_LIMIT = 20 * 1024 * 1024


def params():
    return pltpu.CompilerParams(vmem_limit_bytes=VMEM_LIMIT)


def resident(kernel, name, out_shape, *args, scratch=()):
    spec = pl.BlockSpec(memory_space=pltpu.VMEM)
    return pl.pallas_call(
        kernel,
        out_shape=out_shape,
        in_specs=[spec] * len(args),
        out_specs=jax.tree.map(lambda _: spec, out_shape),
        scratch_shapes=list(scratch),
        compiler_params=params(),
        name=name,
    )(*args)


def lane_iota(shape):
    return lax.broadcasted_iota(jnp.int32, shape, len(shape) - 1)


def nt_dot(a, b):
    return lax.dot_general(a, b, (((1,), (1,)), ((), ())), preferred_element_type=F32)


def nn_dot(a, b):
    return jnp.dot(a, b, preferred_element_type=F32)


def rims_of(rows, head):
    first = RADIUS if head else COLS
    base = RIM + (RADIUS * ROWS if head else 0)
    lane = lane_iota((C, 128))
    total = jnp.zeros((C, 128), F32)
    for r, row in enumerate(rows):
        start = base + RADIUS * r
        moved = pltpu.roll(row, (start - first) % LANES, 1)[:, :128]
        keep = (lane >= start) & (lane < start + RADIUS)
        total = jnp.where(keep, moved, total)
    return total.astype(BF16)


def pack(rows, ref):
    lane = lane_iota((C, 256))
    tails = jnp.zeros((C, 256), F32)
    for k, value in enumerate(rows):
        ref[:, MAIN * k : MAIN * (k + 1)] = value[:, :MAIN].astype(BF16)
        wide = jnp.concatenate([value[:, MAIN:], jnp.zeros((C, 128), F32)], axis=1)
        moved = pltpu.roll(wide, TAIL * k, 1) if k else wide
        keep = (lane >= TAIL * k) & (lane < TAIL * (k + 1))
        tails = jnp.where(keep, moved, tails)
    ref[:, MAIN * RADIUS :] = tails.astype(BF16)


def send_rows(rows, head_ref, tail_ref, up_ref, down_ref):
    pack(rows[:RADIUS], up_ref)
    pack(rows[ROWS - RADIUS :], down_ref)
    head_ref[...] = rims_of(rows, True)
    tail_ref[...] = rims_of(rows, False)


def with_rims(first_tile, last_tile, rims, r):
    lane = lane_iota((C, 128))
    left = pltpu.roll(rims, (-RIM - RADIUS * r) % 128, 1)
    spot = RADIUS + COLS - MAIN
    right = pltpu.roll(rims, (spot - RIM - RADIUS * (ROWS + r)) % 128, 1)
    first_tile = jnp.where(lane < RADIUS, left, first_tile)
    last_tile = jnp.where((lane >= spot) & (lane < spot + RADIUS), right, last_tile)
    return first_tile.astype(BF16), last_tile.astype(BF16)


def fill_own(field_ref, own_ref, rims_ref):
    rims = rims_ref[...].astype(F32)
    for r in range(ROWS):
        first, last = with_rims(
            own_ref[r, :, :128].astype(F32), own_ref[r, :, MAIN:].astype(F32), rims, r
        )
        field_ref[RADIUS + r, :, :128] = first
        field_ref[RADIUS + r, :, 128:MAIN] = own_ref[r, :, 128:MAIN]
        field_ref[RADIUS + r, :, MAIN:] = last


def fill_halo(field_ref, ref, first_row, source_row):
    rims = ref[:, PACK - 128 :].astype(F32)
    tails = ref[:, MAIN * RADIUS :].astype(F32)
    lane = lane_iota((C, 128))
    for k in range(RADIUS):
        moved = pltpu.roll(tails, (-TAIL * k) % 256, 1) if k else tails
        last = jnp.where(lane < TAIL, moved[:, :128], 0.0)
        first, last = with_rims(
            ref[:, MAIN * k : MAIN * k + 128].astype(F32), last, rims, source_row + k
        )
        field_ref[first_row + k, :, :128] = first
        field_ref[first_row + k, :, 128:MAIN] = ref[:, MAIN * k + 128 : MAIN * (k + 1)]
        field_ref[first_row + k, :, MAIN:] = last


def restore_kernel(
    words_ref, low_ref, high_ref, own_ref, head_ref, tail_ref, up_ref, down_ref, bounds
):
    nwords = C // 4
    bounds[...] = jnp.zeros(bounds.shape, F32)
    for g in range(C // GROUP):
        low = low_ref[g].astype(F32)
        bounds[0, g, :, :COLS] = low
        bounds[1, g, :, :COLS] = high_ref[g].astype(F32) - low
    per = GROUP // 4
    row_id = lax.broadcasted_iota(jnp.int32, (C, C), 0)
    col_id = lax.broadcasted_iota(jnp.int32, (C, C), 1)
    place = (row_id == 4 * (col_id % nwords) + col_id // nwords).astype(F32).astype(BF16)
    lane = lane_iota((C, LANES))
    rows = []
    for r in range(ROWS):
        pieces = []
        words = words_ref[:, r, :]
        words = jnp.concatenate([words, jnp.zeros((nwords, LANES - COLS), jnp.int32)], axis=1)
        for j in range(4):
            code = (jnp.right_shift(words, 2 * j) & 3).astype(F32)
            for g in range(C // GROUP):
                low = bounds[0, g, r : r + 1, :]
                span = bounds[1, g, r : r + 1, :]
                value = low + code[g * per : (g + 1) * per] * span / 3.0
                pieces.append(value.astype(BF16))
        mixed = jnp.concatenate(pieces, axis=0)
        value = nn_dot(place, mixed)
        value = pltpu.roll(value, RADIUS, 1)
        value = jnp.where((lane >= RADIUS) & (lane < RADIUS + COLS), value, 0.0)
        rows.append(value)
        own_ref[r] = value.astype(BF16)
    send_rows(rows, head_ref, tail_ref, up_ref, down_ref)


def mlp_kernel(
    words_ref, low_ref, high_ref, grad_ref, scale_ref, w_out_ref, w_in_ref,
    hidden_ref, normed_ref, g_ref, sums_ref,
    order, w_out_p, w_in_p, table, lifted, active,
):
    step = pl.program_id(0)

    @pl.when(step == 0)
    def _():
        row_id = lax.broadcasted_iota(jnp.int32, (FF, FF), 0)
        col_id = lax.broadcasted_iota(jnp.int32, (FF, FF), 1)
        order[...] = (col_id == 4 * (row_id % WORDS) + row_id // WORDS).astype(F32).astype(BF16)
        w_out_p[...] = nt_dot(order[...], w_out_ref[...]).astype(BF16)
        w_in_p[...] = nt_dot(w_in_ref[...], order[...]).astype(BF16)
        g_ref[...] = jnp.zeros((C, FF), F32)
        sums_ref[...] = jnp.zeros((C, 128), F32)

    grad = grad_ref[0].astype(F32)
    scaled = (scale_ref[:, :1] * grad).astype(BF16)
    lifted[...] = nn_dot(w_out_p[...], scaled)
    low = low_ref[0].astype(F32)
    span = high_ref[0].astype(F32) - low
    for k in range(4):
        hidden = low + float(k) * span / 3.0
        cdf = 0.5 * (1.0 + lax.erf(hidden * 0.7071067811865476))
        density = jnp.exp(-0.5 * hidden * hidden) * 0.3989422804014327
        table[k] = hidden * cdf
        table[4 + k] = cdf + hidden * density
    for g in range(FF // GROUP):
        words = words_ref[0, CH * g : CH * (g + 1), :]
        values = [jnp.broadcast_to(table[k, g : g + 1, :], (CH, LANES)) for k in range(8)]
        for j in range(4):
            odd = (words & (1 << (2 * j))) != 0
            upper = (words & (2 << (2 * j))) != 0
            act = jnp.where(
                upper, jnp.where(odd, values[3], values[2]), jnp.where(odd, values[1], values[0])
            )
            slope = jnp.where(
                upper, jnp.where(odd, values[7], values[6]), jnp.where(odd, values[5], values[4])
            )
            place = slice(WORDS * j + CH * g, WORDS * j + CH * (g + 1))
            active[place, :] = act.astype(BF16)
            hidden_ref[0, place, :] = (lifted[place, :] * slope).astype(BF16)
    normed_ref[0] = nn_dot(w_in_p[...], hidden_ref[0])
    g_ref[...] += nt_dot(grad_ref[0], active[...])
    lane = lane_iota((C, 128))
    total = jnp.sum(grad, axis=1, keepdims=True)
    sums_ref[...] += jnp.where(lane == 52, total, 0.0)

    @pl.when(step == ROWS - 1)
    def _():
        value = g_ref[...]
        high = value.astype(BF16)
        rest = (value - high.astype(F32)).astype(BF16)
        g_ref[...] = nn_dot(high, order[...]) + nn_dot(rest, order[...])


def stencil(field_ref, taps_ref, wide_taps, partial, emit, flip):
    def body(block, carry):
        chans = pl.ds(pl.multiple_of(block * CH, CH), CH)
        taps = taps_ref[chans, :]
        for t in range(TAPS * TAPS):
            source = TAPS * TAPS - 1 - t if flip else t
            wide_taps[t] = jnp.broadcast_to(taps[:, source : source + 1], (CH, 128))
        for tile in range(LANES // 128):
            lanes = slice(128 * tile, 128 * (tile + 1))
            cells = [field_ref[r, chans, lanes].astype(F32) for r in range(ROWS + 2 * RADIUS)]
            for q in range(TAPS):
                sums = [None] * ROWS
                for p in range(TAPS):
                    tap = wide_taps[TAPS * p + q]
                    for i in range(ROWS):
                        term = tap * cells[i + p]
                        sums[i] = term if sums[i] is None else sums[i] + term
                for i in range(ROWS):
                    partial[q, i, :, lanes] = sums[i]
        for i in range(ROWS):
            total = partial[0, i]
            for q in range(1, TAPS):
                total = total + pltpu.roll(partial[q, i], LANES - q, 1)
            emit(chans, i, total)
        return carry

    lax.fori_loop(0, C // CH, body, 0)


def conv_kernel(
    own_ref, rims_ref, above_ref, below_ref,
    taps_ref, chan_ref, normed_ref,
    field_ref, grad_ref, head_ref, tail_ref, up_ref, down_ref, normed_in_ref, sums_ref,
    conv, wide_taps, partial,
):
    fill_own(field_ref, own_ref, rims_ref)
    fill_halo(field_ref, above_ref, 0, ROWS - RADIUS)
    fill_halo(field_ref, below_ref, RADIUS + ROWS, 0)

    def emit(chans, i, total):
        conv[i, chans, :] = total + chan_ref[chans, 0:1]

    stencil(field_ref, taps_ref, wide_taps, partial, emit, False)
    gain = chan_ref[:, 1:2]
    bias = chan_ref[:, 2:3]
    lane = lane_iota((C, LANES))
    rows = []
    sum_gain = jnp.zeros((C, LANES), F32)
    sum_bias = jnp.zeros((C, LANES), F32)
    sum_conv = jnp.zeros((C, LANES), F32)
    for r in range(ROWS):
        value = conv[r]
        centered = value - jnp.sum(value, axis=0, keepdims=True) * (1.0 / C)
        variance = jnp.sum(centered * centered, axis=0, keepdims=True) * (1.0 / C)
        inv_std = lax.rsqrt(variance + 1e-06)
        normed = centered * inv_std
        normed_in_ref[r] = (normed * gain + bias).astype(BF16)
        back = normed_ref[r]
        sum_gain = sum_gain + back * normed
        sum_bias = sum_bias + back
        dn = back * gain
        mean_dn = jnp.sum(dn, axis=0, keepdims=True) * (1.0 / C)
        mean_dx = jnp.sum(dn * normed, axis=0, keepdims=True) * (1.0 / C)
        grad = inv_std * (dn - mean_dn - normed * mean_dx)
        grad = jnp.where(lane < COLS, grad, 0.0).astype(BF16).astype(F32)
        sum_conv = sum_conv + grad
        grad = pltpu.roll(grad, RADIUS, 1)
        rows.append(grad)
        grad_ref[r] = grad.astype(BF16)
    send_rows(rows, head_ref, tail_ref, up_ref, down_ref)
    lane = lane_iota((C, 128))
    sums = jnp.where(lane == 49, jnp.sum(sum_gain, axis=1, keepdims=True), 0.0)
    sums = jnp.where(lane == 50, jnp.sum(sum_bias, axis=1, keepdims=True), sums)
    sums_ref[...] = jnp.where(lane == 51, jnp.sum(sum_conv, axis=1, keepdims=True), sums)


def taps_kernel(field_ref, grad_ref, normed_in_ref, hidden_ref, sums_ref, h_ref, order):
    row = lax.broadcasted_iota(jnp.int32, (CH, 256), 0)
    diagonal = lane_iota((CH, 256)) % CH == row
    row = lax.broadcasted_iota(jnp.int32, (128, 128), 0)
    pick = (row // CH == lane_iota((128, 128))).astype(F32).astype(BF16)
    cells = (ROWS + 2 * RADIUS) * CH
    lane = lane_iota((CH, 128))

    def body(block, carry):
        chans = pl.ds(pl.multiple_of(block * CH, CH), CH)
        field = field_ref[:, chans, :].reshape(cells, LANES)
        grads = [grad_ref[i, chans, :] for i in range(ROWS)]
        moved = [
            pltpu.roll(grads[i], (q - RADIUS) % LANES, 1) if q != RADIUS else grads[i]
            for q in range(TAPS)
            for i in range(ROWS)
        ]
        product = nt_dot(jnp.concatenate(moved, axis=0), field)
        product = jnp.concatenate(
            [product, jnp.zeros((TAPS * ROWS * CH, 256 - cells), F32)], axis=1
        )
        totals = []
        for q in range(TAPS):
            total = None
            for i in range(ROWS):
                start = (q * ROWS + i) * CH
                value = jnp.where(diagonal, product[start : start + CH], 0.0)
                value = (pltpu.roll(value, 256 - CH * i, 1) if i else value)[:, :128]
                total = value if total is None else total + value
            totals.append(jnp.where(lane < TAPS * CH, total, 0.0))
        total = jnp.concatenate(totals, axis=0)
        high = total.astype(BF16)
        rest = (total - high.astype(F32)).astype(BF16)
        result = nn_dot(high, pick) + nn_dot(rest, pick)
        sums = jnp.zeros((CH, 128), F32)
        for q in range(TAPS):
            value = result[q * CH : (q + 1) * CH]
            value = pltpu.roll(value, TAPS * q, 1) if q else value
            sums = jnp.where((lane >= TAPS * q) & (lane < TAPS * (q + 1)), value, sums)
        sums_ref[chans, :] = sums
        return carry

    lax.fori_loop(0, C // CH, body, 0, unroll=2)
    h_sum = jnp.zeros((C, FF), F32)
    for r in range(ROWS):
        h_sum = h_sum + nt_dot(normed_in_ref[r], hidden_ref[r])
    row_id = lax.broadcasted_iota(jnp.int32, (FF, FF), 0)
    col_id = lax.broadcasted_iota(jnp.int32, (FF, FF), 1)
    order[...] = (col_id == 4 * (row_id % WORDS) + row_id // WORDS).astype(F32).astype(BF16)
    high = h_sum.astype(BF16)
    rest = (h_sum - high.astype(F32)).astype(BF16)
    h_ref[...] = nn_dot(high, order[...]) + nn_dot(rest, order[...])


def input_kernel(
    own_ref, rims_ref, above_ref, below_ref, taps_ref, grad_ref,
    out_ref, field, wide_taps, partial,
):
    fill_own(field, own_ref, rims_ref)
    fill_halo(field, above_ref, 0, ROWS - RADIUS)
    fill_halo(field, below_ref, RADIUS + ROWS, 0)

    def emit(chans, i, total):
        out_ref[i, chans, :] = (grad_ref[i, chans, :].astype(F32) + total).astype(BF16)

    stencil(field, taps_ref, wide_taps, partial, emit, True)


def ring(axis, count):
    ahead = [(i, (i + 1) % count) for i in range(count)]
    return functools.partial(lax.ppermute, axis_name=axis, perm=ahead), functools.partial(
        lax.ppermute, axis_name=axis, perm=[(b, a) for a, b in ahead]
    )


def extend(head, tail, up, down):
    ahead, behind = ring("lon", lax.axis_size("lon"))
    rims = ahead(tail) + behind(head)
    up = jnp.concatenate([up[:, : PACK - 128], up[:, PACK - 128 :] + rims], axis=1)
    down = jnp.concatenate([down[:, : PACK - 128], down[:, PACK - 128 :] + rims], axis=1)
    count = lax.axis_size("lat")
    above = lax.ppermute(down, "lat", [(i, i + 1) for i in range(count - 1)])
    below = lax.ppermute(up, "lat", [(i + 1, i) for i in range(count - 1)])
    return rims, above, below, up


def swap(value, bit):
    count = lax.axis_size("lat") * lax.axis_size("lon")
    return lax.ppermute(value, ("lat", "lon"), [(i, i ^ bit) for i in range(count)])


def rounded(value):
    return lax.reduce_precision(value, 8, 7)


def all_sum(value, tied, step):
    me = lax.axis_index("lat") * lax.axis_size("lon") + lax.axis_index("lon")
    split = (1, 4, 8)
    whole = (32, 64, 2, 16)
    for count, bit in enumerate(split):
        if count == step:
            value, tied = lax.optimization_barrier((value, tied))
        half = value.shape[0] // 2
        upper = (me & bit) != 0
        low, high = value[:half], value[half:]
        send = jnp.where(upper, low, high)
        keep = jnp.where(upper, high, low)
        value = keep + swap(send.astype(BF16) if bit > 1 else send, bit).astype(F32)
    for count, bit in enumerate(whole):
        if count + len(split) == step:
            value, tied = lax.optimization_barrier((value, tied))
        sent = rounded(value)
        value = sent + swap(sent.astype(BF16), bit).astype(F32)
    value = rounded(value).astype(BF16)
    for bit in reversed(split):
        upper = (me & bit) != 0
        other = swap(value, bit)
        value = jnp.concatenate(
            [jnp.where(upper, other, value), jnp.where(upper, value, other)], axis=0
        )
    return value.astype(F32), tied


def by_row(array):
    moved = jnp.transpose(array, (1, 0, 2))
    return jnp.pad(moved, ((0, 0), (0, 0), (0, LANES - moved.shape[2])))


def local(
    stash_input, input_low, input_high, stash_hidden, hidden_low, hidden_high, grad_out,
    kernel, conv_bias, norm_gain, norm_bias, w_in, w_out, out_bias, layer_scale,
):
    field_shape = jax.ShapeDtypeStruct((ROWS, C, LANES), BF16)
    rim_shape = jax.ShapeDtypeStruct((C, 128), BF16)
    pack_shape = jax.ShapeDtypeStruct((C, PACK), BF16)
    own, *sends = resident(
        restore_kernel,
        "restore",
        (field_shape, rim_shape, rim_shape, pack_shape, pack_shape),
        stash_input,
        input_low,
        input_high,
        scratch=[pltpu.VMEM((2, C // GROUP, ROWS, LANES), F32)],
    )
    *halo, _ = extend(*sends)

    taps = jnp.pad(kernel.reshape(C, TAPS * TAPS), ((0, 0), (0, 128 - TAPS * TAPS)))
    chan = jnp.stack([conv_bias, norm_gain, norm_bias, layer_scale, out_bias], axis=1)
    chan = jnp.pad(chan, ((0, 0), (0, 123)))
    grad_rows = by_row(grad_out)

    def row_spec(count):
        return pl.BlockSpec((1, count, LANES), lambda r: (r, 0, 0))

    def whole_spec(*shape):
        return pl.BlockSpec(shape, lambda r: (0,) * len(shape))

    scale_wide = jnp.broadcast_to(layer_scale[:, None], (C, 128))
    hidden_back, normed_back, g_part, sums_a = pl.pallas_call(
        mlp_kernel,
        grid=(ROWS,),
        in_specs=[
            row_spec(WORDS), row_spec(FF // GROUP), row_spec(FF // GROUP), row_spec(C),
            whole_spec(C, 128), whole_spec(C, FF), whole_spec(C, FF),
        ],
        out_specs=[row_spec(FF), row_spec(C), whole_spec(C, FF), whole_spec(C, 128)],
        out_shape=(
            jax.ShapeDtypeStruct((ROWS, FF, LANES), BF16),
            jax.ShapeDtypeStruct((ROWS, C, LANES), F32),
            jax.ShapeDtypeStruct((C, FF), F32),
            jax.ShapeDtypeStruct((C, 128), F32),
        ),
        scratch_shapes=[
            pltpu.VMEM((FF, FF), BF16),
            pltpu.VMEM((FF, C), BF16),
            pltpu.VMEM((C, FF), BF16),
            pltpu.VMEM((8, FF // GROUP, LANES), F32),
            pltpu.VMEM((FF, LANES), F32),
            pltpu.VMEM((FF, LANES), BF16),
        ],
        compiler_params=params(),
        name="mlp",
    )(
        by_row(stash_hidden), by_row(hidden_low), by_row(hidden_high), grad_rows,
        scale_wide, jnp.transpose(w_out), w_in,
    )

    stencil_scratch = [
        pltpu.VMEM((TAPS * TAPS, CH, 128), F32),
        pltpu.VMEM((TAPS, ROWS, CH, LANES), F32),
    ]
    field, grad_own, *sends, normed_in, sums_b = resident(
        conv_kernel,
        "conv",
        (
            jax.ShapeDtypeStruct((ROWS + 2 * RADIUS, C, LANES), BF16),
            field_shape,
            rim_shape,
            rim_shape,
            pack_shape,
            pack_shape,
            field_shape,
            jax.ShapeDtypeStruct((C, 128), F32),
        ),
        own,
        *halo,
        taps,
        chan,
        normed_back,
        scratch=[pltpu.VMEM((ROWS, C, LANES), F32)] + stencil_scratch,
    )

    *grad_halo, _ = extend(*sends)
    sums_c, h_part = resident(
        taps_kernel,
        "taps",
        (jax.ShapeDtypeStruct((C, 128), F32), jax.ShapeDtypeStruct((C, FF), F32)),
        field,
        grad_own,
        normed_in,
        hidden_back,
        scratch=[pltpu.VMEM((FF, FF), BF16)],
    )
    total, grad_halo = all_sum(
        jnp.concatenate([g_part, h_part, sums_a + sums_b + sums_c], axis=1), grad_halo, TIE
    )
    grad_input = resident(
        input_kernel,
        "input",
        field_shape,
        grad_own,
        *grad_halo,
        taps,
        grad_rows,
        scratch=[pltpu.VMEM((ROWS + 2 * RADIUS, C, LANES), BF16)] + stencil_scratch,
    )
    grad_input = jnp.transpose(grad_input[:, :, :COLS], (1, 0, 2))

    cells = ROWS * lax.axis_size("lat") * COLS * lax.axis_size("lon")
    factor = 1.0 / math.sqrt(cells)
    total = total * factor
    g_sum, h_sum, sums = total[:, :FF], total[:, FF : 2 * FF], total[:, 2 * FF :]
    sum_grad = sums[:, 52]
    grad_scale = jnp.sum(g_sum * jnp.transpose(w_out).astype(F32), axis=1) + out_bias * sum_grad
    return (
        grad_input,
        jnp.transpose(sums[:, : TAPS * TAPS].reshape(C, TAPS, TAPS), (0, 2, 1)),
        sums[:, 51],
        sums[:, 49],
        sums[:, 50],
        h_sum,
        jnp.transpose(g_sum * layer_scale[:, None]),
        sum_grad * layer_scale,
        grad_scale,
    )


def solution(mesh):
    split = P(None, "lat", "lon")
    return jax.shard_map(
        local,
        mesh=mesh,
        in_specs=(split,) * 7 + (P(),) * 8,
        out_specs=(split,) + (P(),) * 8,
        check_vma=False,
    )
```

```python
import functools
import math

import jax
import jax.numpy as jnp
from jax import lax
from jax.experimental import pallas as pl
from jax.experimental.pallas import tpu as pltpu
from jax.sharding import PartitionSpec as P

C = 192
FF = 768
WORDS = FF // 4
GROUP = 64
RADIUS = 3
TAPS = 2 * RADIUS + 1
ROWS = 4
COLS = 450
WIDE = COLS + 2 * RADIUS
LANES = 512
MAIN = 384
TAIL = COLS + RADIUS - MAIN
PACK = 1408
RIM = MAIN * RADIUS + TAIL * RADIUS - (PACK - 128)
CH = 16
F32 = jnp.float32
BF16 = jnp.bfloat16
VMEM_LIMIT = 18 * 1024 * 1024


def params():
    return pltpu.CompilerParams(vmem_limit_bytes=VMEM_LIMIT)


def resident(kernel, name, out_shape, *args, scratch=(), space=pltpu.VMEM, aliases=()):
    spec = pl.BlockSpec(memory_space=pltpu.VMEM)
    return pl.pallas_call(
        kernel,
        out_shape=out_shape,
        in_specs=[pl.BlockSpec(memory_space=space)] * len(args),
        out_specs=jax.tree.map(lambda _: spec, out_shape),
        scratch_shapes=list(scratch),
        input_output_aliases=dict(aliases),
        cost_estimate=pl.CostEstimate(flops=0, bytes_accessed=0, transcendentals=0),
        compiler_params=params(),
        name=name,
    )(*args)


def lane_iota(shape):
    return lax.broadcasted_iota(jnp.int32, shape, len(shape) - 1)


def nt_dot(a, b):
    return lax.dot_general(a, b, (((1,), (1,)), ((), ())), preferred_element_type=F32)


def nn_dot(a, b):
    return jnp.dot(a, b, preferred_element_type=F32)


def rims_of(rows, head):
    first = RADIUS if head else COLS
    base = RIM + (RADIUS * ROWS if head else 0)
    lane = lane_iota((C, 128))
    total = jnp.zeros((C, 128), F32)
    for r, row in enumerate(rows):
        start = base + RADIUS * r
        moved = pltpu.roll(row, (start - first) % LANES, 1)[:, :128]
        keep = (lane >= start) & (lane < start + RADIUS)
        total = jnp.where(keep, moved, total)
    return total.astype(BF16)


def pack(rows, ref):
    lane = lane_iota((C, 256))
    tails = jnp.zeros((C, 256), F32)
    for k, value in enumerate(rows):
        ref[:, MAIN * k : MAIN * (k + 1)] = value[:, :MAIN].astype(BF16)
        wide = jnp.concatenate([value[:, MAIN:], jnp.zeros((C, 128), F32)], axis=1)
        moved = pltpu.roll(wide, TAIL * k, 1) if k else wide
        keep = (lane >= TAIL * k) & (lane < TAIL * (k + 1))
        tails = jnp.where(keep, moved, tails)
    ref[:, MAIN * RADIUS :] = tails.astype(BF16)


def send_rows(rows, head_ref, tail_ref, up_ref, down_ref):
    pack(rows[:RADIUS], up_ref)
    pack(rows[ROWS - RADIUS :], down_ref)
    head_ref[...] = rims_of(rows, True)
    tail_ref[...] = rims_of(rows, False)


def with_rims(first_tile, last_tile, rims, r):
    lane = lane_iota((C, 128))
    left = pltpu.roll(rims, (-RIM - RADIUS * r) % 128, 1)
    spot = RADIUS + COLS - MAIN
    right = pltpu.roll(rims, (spot - RIM - RADIUS * (ROWS + r)) % 128, 1)
    first_tile = jnp.where(lane < RADIUS, left, first_tile)
    last_tile = jnp.where((lane >= spot) & (lane < spot + RADIUS), right, last_tile)
    return first_tile.astype(BF16), last_tile.astype(BF16)


def fill_halo(field_ref, ref, first_row, source_row):
    rims = ref[:, PACK - 128 :].astype(F32)
    tails = ref[:, MAIN * RADIUS :].astype(F32)
    lane = lane_iota((C, 128))
    for k in range(RADIUS):
        moved = pltpu.roll(tails, (-TAIL * k) % 256, 1) if k else tails
        last = jnp.where(lane < TAIL, moved[:, :128], 0.0)
        first, last = with_rims(
            ref[:, MAIN * k : MAIN * k + 128].astype(F32), last, rims, source_row + k
        )
        field_ref[first_row + k, :, :128] = first
        field_ref[first_row + k, :, 128:MAIN] = ref[:, MAIN * k + 128 : MAIN * (k + 1)]
        field_ref[first_row + k, :, MAIN:] = last


def fetch(sources, targets, sems, meanwhile=None):
    copies = [
        pltpu.make_async_copy(source, target, sems.at[k])
        for k, (source, target) in enumerate(zip(sources, targets))
    ]
    for copy in copies:
        copy.start()
    if meanwhile is not None:
        meanwhile()
    for copy in copies:
        copy.wait()


def restore_kernel(
    words_hbm, low_hbm, high_hbm, own_ref, head_ref, tail_ref, up_ref, down_ref,
    words_ref, low_ref, high_ref, bounds, sems,
):
    fetch((words_hbm, low_hbm, high_hbm), (words_ref, low_ref, high_ref), sems)
    nwords = C // 4
    bounds[...] = jnp.zeros(bounds.shape, F32)
    for g in range(C // GROUP):
        low = low_ref[g].astype(F32)
        bounds[0, g, :, :COLS] = low
        bounds[1, g, :, :COLS] = high_ref[g].astype(F32) - low
    per = GROUP // 4
    row_id = lax.broadcasted_iota(jnp.int32, (C, C), 0)
    col_id = lax.broadcasted_iota(jnp.int32, (C, C), 1)
    place = (row_id == 4 * (col_id % nwords) + col_id // nwords).astype(F32).astype(BF16)
    lane = lane_iota((C, LANES))
    rows = []
    for r in range(ROWS):
        pieces = []
        words = words_ref[:, r, :]
        words = jnp.concatenate([words, jnp.zeros((nwords, LANES - COLS), jnp.int32)], axis=1)
        for j in range(4):
            code = (jnp.right_shift(words, 2 * j) & 3).astype(F32)
            for g in range(C // GROUP):
                low = bounds[0, g, r : r + 1, :]
                span = bounds[1, g, r : r + 1, :]
                value = low + code[g * per : (g + 1) * per] * span / 3.0
                pieces.append(value.astype(BF16))
        mixed = jnp.concatenate(pieces, axis=0)
        value = nn_dot(place, mixed)
        value = pltpu.roll(value, RADIUS, 1)
        value = jnp.where((lane >= RADIUS) & (lane < RADIUS + COLS), value, 0.0)
        rows.append(value)
        own_ref[r] = value.astype(BF16)
    send_rows(rows, head_ref, tail_ref, up_ref, down_ref)


def natural_order(order):
    row_id = lax.broadcasted_iota(jnp.int32, (FF, FF), 0)
    col_id = lax.broadcasted_iota(jnp.int32, (FF, FF), 1)
    order[...] = (col_id == 4 * (row_id % WORDS) + row_id // WORDS).astype(F32).astype(BF16)


def reorder(value, order):
    high = value.astype(BF16)
    rest = (value - high.astype(F32)).astype(BF16)
    return nn_dot(high, order[...]) + nn_dot(rest, order[...])


def mlp_kernel(
    words_hbm, low_hbm, high_hbm, grad_hbm, chan_hbm, w_out_hbm, w_in_hbm,
    hidden_ref, normed_ref, g_ref, sums_ref, rows_ref,
    words_ref, low_ref, high_ref, grad_ref, chan_ref, w_out_ref, w_in_ref, sems,
    order, w_out_p, w_in_p, lifted, active, bounds, grads,
):
    fetch(
        (w_out_hbm, w_in_hbm, low_hbm, high_hbm, grad_hbm, words_hbm, chan_hbm),
        (w_out_ref, w_in_ref, low_ref, high_ref, grad_ref, words_ref, chan_ref),
        sems,
        functools.partial(natural_order, order),
    )
    w_out_p[...] = nt_dot(order[...], w_out_ref[...]).astype(BF16)
    w_in_p[...] = nt_dot(w_in_ref[...], order[...]).astype(BF16)
    groups = FF // GROUP
    bounds[...] = jnp.zeros(bounds.shape, F32)
    grads[...] = grad_ref[...].astype(F32)
    for g in range(groups):
        low = low_ref[g].astype(F32)
        span = high_ref[g].astype(F32) - low
        for k in range(4):
            hidden = low + float(k) * span / 3.0
            cdf = 0.5 * (1.0 + lax.erf(hidden * 0.7071067811865476))
            density = jnp.exp(-0.5 * hidden * hidden) * 0.3989422804014327
            bounds[k, g, :, :COLS] = hidden * cdf
            bounds[4 + k, g, :, :COLS] = cdf + hidden * density
    g_sum = jnp.zeros((C, FF), F32)
    total = jnp.zeros((C, 1), F32)
    for r in range(ROWS):
        grad = grads[:, r, :]
        grad = jnp.concatenate([grad, jnp.zeros((C, LANES - COLS), F32)], axis=1)
        total = total + jnp.sum(grad, axis=1, keepdims=True)
        rows_ref[r] = grad.astype(BF16)
        scaled = (chan_ref[:, 3:4] * grad).astype(BF16)
        lifted[...] = nn_dot(w_out_p[...], scaled)
        words_row = words_ref[:, r, :]
        words_row = jnp.concatenate(
            [words_row, jnp.zeros((WORDS, LANES - COLS), jnp.int32)], axis=1
        )
        for g in range(groups):
            words = words_row[CH * g : CH * (g + 1)]
            values = [
                jnp.broadcast_to(bounds[k, g, r : r + 1, :], (CH, LANES)) for k in range(8)
            ]
            for j in range(4):
                odd = (words & (1 << (2 * j))) != 0
                upper = (words & (2 << (2 * j))) != 0
                act = jnp.where(
                    upper,
                    jnp.where(odd, values[3], values[2]),
                    jnp.where(odd, values[1], values[0]),
                )
                slope = jnp.where(
                    upper,
                    jnp.where(odd, values[7], values[6]),
                    jnp.where(odd, values[5], values[4]),
                )
                place = slice(WORDS * j + CH * g, WORDS * j + CH * (g + 1))
                active[place, :] = act.astype(BF16)
                hidden_ref[r, place, :] = (lifted[place, :] * slope).astype(BF16)
        normed_ref[r] = nn_dot(w_in_p[...], hidden_ref[r])
        g_sum = g_sum + nt_dot(rows_ref[r], active[...])
    sums_ref[...] = jnp.where(lane_iota((C, 128)) == 52, total, 0.0)
    g_ref[...] = reorder(g_sum, order)


OWN = tuple(range(RADIUS, RADIUS + ROWS))
HALO = tuple(range(RADIUS)) + tuple(range(RADIUS + ROWS, 2 * RADIUS + ROWS))


def stencil(cell, used, taps_ref, wide_taps, partial, emit, flip):
    def body(block, carry):
        chans = pl.ds(pl.multiple_of(block * CH, CH), CH)
        taps = taps_ref[chans, :]
        for t in range(TAPS * TAPS):
            source = TAPS * TAPS - 1 - t if flip else t
            wide_taps[t] = jnp.broadcast_to(taps[:, source : source + 1], (CH, 128))
        for tile in range(LANES // 128):
            lanes = slice(128 * tile, 128 * (tile + 1))
            cells = {r: cell(r, chans, lanes).astype(F32) for r in used}
            for q in range(TAPS):
                sums = [None] * ROWS
                for p in range(TAPS):
                    tap = wide_taps[TAPS * p + q]
                    for i in range(ROWS):
                        if i + p in cells:
                            term = tap * cells[i + p]
                            sums[i] = term if sums[i] is None else sums[i] + term
                for i in range(ROWS):
                    partial[q, i, :, lanes] = sums[i]
        for i in range(ROWS):
            total = partial[0, i]
            for q in range(1, TAPS):
                total = total + pltpu.roll(partial[q, i], LANES - q, 1)
            emit(chans, i, total)
        return carry

    lax.fori_loop(0, C // CH, body, 0)


def own_kernel(own_ref, rims_ref, taps_ref, filled_ref, total_ref, wide_taps, partial, *, flip):
    rims = rims_ref[...].astype(F32)
    for r in range(ROWS):
        first, last = with_rims(
            own_ref[r, :, :128].astype(F32), own_ref[r, :, MAIN:].astype(F32), rims, r
        )
        filled_ref[r, :, :128] = first
        filled_ref[r, :, 128:MAIN] = own_ref[r, :, 128:MAIN]
        filled_ref[r, :, MAIN:] = last

    def emit(chans, i, total):
        total_ref[i, chans, :] = total

    def cell(r, chans, lanes):
        return filled_ref[r - RADIUS, chans, lanes]

    stencil(cell, OWN, taps_ref, wide_taps, partial, emit, flip)


def conv_kernel(
    filled_ref, total_ref, above_ref, below_ref, taps_ref, chan_ref, normed_ref,
    field_ref, grad_ref, head_ref, tail_ref, up_ref, down_ref, normed_in_ref, sums_ref,
    conv, sums, wide_taps, partial,
):
    fill_halo(field_ref, above_ref, 0, ROWS - RADIUS)
    fill_halo(field_ref, below_ref, RADIUS + ROWS, 0)
    field_ref[RADIUS : RADIUS + ROWS] = filled_ref[...]

    def emit(chans, i, total):
        conv[i, chans, :] = total_ref[i, chans, :] + (total + chan_ref[chans, 0:1])

    def cell(r, chans, lanes):
        return field_ref[r, chans, lanes]

    stencil(cell, HALO, taps_ref, wide_taps, partial, emit, False)
    gain = jnp.broadcast_to(chan_ref[:, 1:2], (C, 128))
    bias = jnp.broadcast_to(chan_ref[:, 2:3], (C, 128))
    sums[...] = jnp.zeros(sums.shape, F32)
    rows = []
    for r in range(ROWS):
        for tile in range(LANES // 128):
            lanes = slice(128 * tile, 128 * (tile + 1))
            value = conv[r, :, lanes]
            centered = value - jnp.sum(value, axis=0, keepdims=True) * (1.0 / C)
            variance = jnp.sum(centered * centered, axis=0, keepdims=True) * (1.0 / C)
            inv_std = lax.rsqrt(variance + 1e-06)
            normed = centered * inv_std
            normed_in_ref[r, :, lanes] = (normed * gain + bias).astype(BF16)
            back = normed_ref[r, :, lanes]
            sums[0] += back * normed
            sums[1] += back
            dn = back * gain
            mean_dn = jnp.sum(dn, axis=0, keepdims=True) * (1.0 / C)
            mean_dx = jnp.sum(dn * normed, axis=0, keepdims=True) * (1.0 / C)
            grad = inv_std * (dn - mean_dn - normed * mean_dx)
            if 128 * (tile + 1) > COLS:
                grad = jnp.where(lane_iota((C, 128)) < COLS - 128 * tile, grad, 0.0)
            grad = grad.astype(BF16).astype(F32)
            sums[2] += grad
            conv[r, :, lanes] = grad
        grad = pltpu.roll(conv[r], RADIUS, 1)
        rows.append(grad)
        grad_ref[r] = grad.astype(BF16)
    send_rows(rows, head_ref, tail_ref, up_ref, down_ref)
    lane = lane_iota((C, 128))
    total = jnp.zeros((C, 128), F32)
    for k in range(3):
        total = jnp.where(lane == 49 + k, jnp.sum(sums[k], axis=1, keepdims=True), total)
    sums_ref[...] = total


def taps_kernel(field_ref, grad_ref, normed_in_ref, hidden_ref, sums_ref, h_ref, order):
    row = lax.broadcasted_iota(jnp.int32, (CH, 256), 0)
    diagonal = lane_iota((CH, 256)) % CH == row
    row = lax.broadcasted_iota(jnp.int32, (128, 128), 0)
    pick = (TAPS * (row // CH) == lane_iota((128, 128))).astype(F32).astype(BF16)
    cells = (ROWS + 2 * RADIUS) * CH
    lane = lane_iota((CH, 128))

    def body(block, carry):
        chans = pl.ds(pl.multiple_of(block * CH, CH), CH)
        field = field_ref[:, chans, :].reshape(cells, LANES)
        grads = [grad_ref[i, chans, :] for i in range(ROWS)]
        moved = [
            pltpu.roll(grads[i], (q - RADIUS) % LANES, 1) if q != RADIUS else grads[i]
            for q in range(TAPS)
            for i in range(ROWS)
        ]
        product = nt_dot(jnp.concatenate(moved, axis=0), field)
        product = jnp.concatenate(
            [product, jnp.zeros((TAPS * ROWS * CH, 256 - cells), F32)], axis=1
        )
        totals = []
        for q in range(TAPS):
            total = None
            for i in range(ROWS):
                start = (q * ROWS + i) * CH
                value = jnp.where(diagonal, product[start : start + CH], 0.0)
                value = (pltpu.roll(value, 256 - CH * i, 1) if i else value)[:, :128]
                total = value if total is None else total + value
            totals.append(jnp.where(lane < TAPS * CH, total, 0.0))
        total = jnp.concatenate(totals, axis=0)
        high = total.astype(BF16)
        rest = (total - high.astype(F32)).astype(BF16)
        result = nn_dot(high, pick) + nn_dot(rest, pick)
        sums = jnp.zeros((CH, 128), F32)
        for q in range(TAPS):
            value = result[q * CH : (q + 1) * CH]
            value = pltpu.roll(value, q, 1) if q else value
            sums = jnp.where(lane % TAPS == q, value, sums)
        sums = jnp.where(lane < TAPS * TAPS, sums, 0.0)
        sums_ref[chans, :] = sums
        return carry

    lax.fori_loop(0, C // CH, body, 0, unroll=2)
    natural_order(order)
    h_sum = jnp.zeros((C, FF), F32)
    for r in range(ROWS):
        h_sum = h_sum + nt_dot(normed_in_ref[r], hidden_ref[r])
    h_ref[...] = reorder(h_sum, order)


def input_kernel(
    total_ref, above_ref, below_ref, taps_ref, grad_ref, out_ref, field, wide_taps, partial
):
    fill_halo(field, above_ref, 0, ROWS - RADIUS)
    fill_halo(field, below_ref, RADIUS, 0)

    def emit(chans, i, total):
        total = total + total_ref[i, chans, :]
        out_ref[i, chans, :] = (grad_ref[i, chans, :].astype(F32) + total).astype(BF16)

    def cell(r, chans, lanes):
        return field[r if r < RADIUS else r - ROWS, chans, lanes]

    stencil(cell, HALO, taps_ref, wide_taps, partial, emit, True)


def final_kernel(total_ref, chan_ref, w_out_ref, g_ref, h_ref, taps_ref, vectors_ref, *, factor):
    g_sum = total_ref[:, :FF].astype(F32) * factor
    h_ref[...] = total_ref[:, FF : 2 * FF].astype(F32) * factor
    sums = total_ref[:, 2 * FF :].astype(F32) * factor
    scale = chan_ref[:, 3:4]
    g_ref[...] = g_sum * scale
    total = jnp.sum(g_sum * w_out_ref[...].astype(F32), axis=1, keepdims=True)
    sum_grad = sums[:, 52:53]
    lane = lane_iota((C, 128))
    sums = jnp.where(lane == 53, total + chan_ref[:, 4:5] * sum_grad, sums)
    sums = jnp.where(lane == 52, sum_grad * scale, sums)
    flat = jnp.transpose(sums)
    for p in range(TAPS):
        taps_ref[p] = flat[TAPS * p : TAPS * (p + 1)]
    vectors_ref[...] = flat[48:56]


def ring(axis, count):
    ahead = [(i, (i + 1) % count) for i in range(count)]
    return functools.partial(lax.ppermute, axis_name=axis, perm=ahead), functools.partial(
        lax.ppermute, axis_name=axis, perm=[(b, a) for a, b in ahead]
    )


def add_rims(head, tail, up, down):
    ahead, behind = ring("lon", lax.axis_size("lon"))
    rims = ahead(tail) + behind(head)
    up = jnp.concatenate([up[:, : PACK - 128], up[:, PACK - 128 :] + rims], axis=1)
    down = jnp.concatenate([down[:, : PACK - 128], down[:, PACK - 128 :] + rims], axis=1)
    return rims, up, down


def lat_rows(up, down):
    count = lax.axis_size("lat")
    above = lax.ppermute(down, "lat", [(i, i + 1) for i in range(count - 1)])
    below = lax.ppermute(up, "lat", [(i + 1, i) for i in range(count - 1)])
    return above, below


def swap(value, bits):
    count = lax.axis_size("lat") * lax.axis_size("lon")
    return lax.ppermute(value, ("lat", "lon"), [(i, i ^ bits) for i in range(count)])


def rounded(value):
    return lax.reduce_precision(value, 8, 7)


def all_sum(value, hooks):
    me = lax.axis_index("lat") * lax.axis_size("lon") + lax.axis_index("lon")
    split = (1, 4, 8)
    step = 0
    for bit in split:
        value = hooks(step, value)
        step += 1
        half = value.shape[0] // 2
        upper = (me & bit) != 0
        low, high = value[:half], value[half:]
        send = jnp.where(upper, low, high)
        keep = jnp.where(upper, high, low)
        value = keep + swap(send.astype(BF16) if bit > 1 else send, bit).astype(F32)
    for first, second in ((32, 64), (2, 16)):
        value = hooks(step, value)
        step += 1
        mine = rounded(value)
        sent = mine.astype(BF16)
        near, far, both = (swap(sent, b).astype(F32) for b in (first, second, first | second))
        value = (mine + near) + (far + both)
    value = rounded(value).astype(BF16)
    for bit in reversed(split):
        value = hooks(step, value)
        step += 1
        upper = (me & bit) != 0
        other = swap(value, bit)
        value = jnp.concatenate(
            [jnp.where(upper, other, value), jnp.where(upper, value, other)], axis=0
        )
    return hooks(step, value)


def local(
    stash_input, input_low, input_high, stash_hidden, hidden_low, hidden_high, grad_out,
    kernel, conv_bias, norm_gain, norm_bias, w_in, w_out, out_bias, layer_scale,
):
    tie = lax.optimization_barrier

    def shape(*dims, dtype=F32):
        return jax.ShapeDtypeStruct(dims, dtype)

    field_shape = shape(ROWS, C, LANES, dtype=BF16)
    total_shape = shape(ROWS, C, LANES)
    rim_shape = shape(C, 128, dtype=BF16)
    pack_shape = shape(C, PACK, dtype=BF16)
    sums_shape = shape(C, 128)
    weight_shape = shape(C, FF)
    own, head, tail, up, down = resident(
        restore_kernel,
        "restore",
        (field_shape, rim_shape, rim_shape, pack_shape, pack_shape),
        stash_input,
        input_low,
        input_high,
        scratch=[
            pltpu.VMEM(stash_input.shape, jnp.int32),
            pltpu.VMEM(input_low.shape, BF16),
            pltpu.VMEM(input_high.shape, BF16),
            pltpu.VMEM((2, C // GROUP, ROWS, LANES), F32),
            pltpu.SemaphoreType.DMA((3,)),
        ],
        space=pl.ANY,
    )
    rims, up, down = add_rims(head, tail, up, down)
    above, below = lat_rows(up, down)

    taps = jnp.pad(kernel.reshape(C, TAPS * TAPS), ((0, 0), (0, 128 - TAPS * TAPS)))
    chan = jnp.stack([conv_bias, norm_gain, norm_bias, layer_scale, out_bias], axis=1)
    chan = jnp.pad(chan, ((0, 0), (0, 123)))
    w_out_t = jnp.transpose(w_out)
    stencil_scratch = [
        pltpu.VMEM((TAPS * TAPS, CH, 128), F32),
        pltpu.VMEM((TAPS, ROWS, CH, LANES), F32),
    ]
    hidden_back, normed_back, g_part, sums_a, grad_rows = resident(
        mlp_kernel,
        "mlp",
        (
            shape(ROWS, FF, LANES, dtype=BF16),
            total_shape,
            weight_shape,
            sums_shape,
            field_shape,
        ),
        stash_hidden,
        hidden_low,
        hidden_high,
        grad_out,
        chan,
        w_out_t,
        w_in,
        space=pl.ANY,
        scratch=[
            pltpu.VMEM(stash_hidden.shape, jnp.int32),
            pltpu.VMEM(hidden_low.shape, BF16),
            pltpu.VMEM(hidden_high.shape, BF16),
            pltpu.VMEM(grad_out.shape, BF16),
            pltpu.VMEM(chan.shape, F32),
            pltpu.VMEM((C, FF), BF16),
            pltpu.VMEM((C, FF), BF16),
            pltpu.SemaphoreType.DMA((7,)),
            pltpu.VMEM((FF, FF), BF16),
            pltpu.VMEM((FF, C), BF16),
            pltpu.VMEM((C, FF), BF16),
            pltpu.VMEM((FF, LANES), F32),
            pltpu.VMEM((FF, LANES), BF16),
            pltpu.VMEM((8, FF // GROUP, ROWS, LANES), F32),
            pltpu.VMEM(grad_out.shape, F32),
        ],
    )

    def over_own(own, rims, flip, name):
        return resident(
            functools.partial(own_kernel, flip=flip),
            name,
            (field_shape, total_shape),
            own,
            rims,
            taps,
            scratch=stencil_scratch,
        )

    filled, total = over_own(own, rims, False, "conv_own")
    field, grad_own, head, tail, up, down, normed_in, sums_b = resident(
        conv_kernel,
        "conv",
        (
            shape(ROWS + 2 * RADIUS, C, LANES, dtype=BF16),
            field_shape,
            rim_shape,
            rim_shape,
            pack_shape,
            pack_shape,
            field_shape,
            sums_shape,
        ),
        filled,
        total,
        above,
        below,
        taps,
        chan,
        normed_back,
        scratch=[pltpu.VMEM((ROWS, C, LANES), F32), pltpu.VMEM((3, C, 128), F32)]
        + stencil_scratch,
    )

    sums_c, h_part = resident(
        taps_kernel,
        "taps",
        (sums_shape, weight_shape),
        field,
        grad_own,
        normed_in,
        hidden_back,
        scratch=[pltpu.VMEM((FF, FF), BF16)],
    )
    rims, up, down = add_rims(head, tail, up, down)
    above, below = lat_rows(up, down)
    late = {"own": grad_own, "above": above, "below": below}

    def hooks(step, value):
        if step == 1:
            value, late["own"] = tie((value, late["own"]))
            late["total"] = over_own(late["own"], rims, True, "input_own")[1]
        elif step == 2:
            value, late["total"] = tie((value, late["total"]))
        elif step == 3:
            value, late["total"], late["above"], late["below"] = tie(
                (value, late["total"], late["above"], late["below"])
            )
        elif step == 5:
            value, late["total"] = tie((value, late["total"]))
            late["input"] = resident(
                input_kernel,
                "input",
                field_shape,
                late["total"],
                late["above"],
                late["below"],
                taps,
                grad_rows,
                scratch=[pltpu.VMEM((2 * RADIUS, C, LANES), BF16)] + stencil_scratch,
            )
        elif step == 6:
            value, late["input"] = tie((value, late["input"]))
            late["input"] = jnp.transpose(late["input"][:, :, :COLS], (1, 0, 2))
        elif step == 7:
            value, late["input"] = tie((value, late["input"]))
        return value

    summed = all_sum(jnp.concatenate([g_part, h_part, sums_a + sums_b + sums_c], axis=1), hooks)
    cells = ROWS * lax.axis_size("lat") * COLS * lax.axis_size("lon")
    g_sum, h_sum, grad_kernel, vectors = resident(
        functools.partial(final_kernel, factor=1.0 / math.sqrt(cells)),
        "final",
        (weight_shape, weight_shape, shape(TAPS, TAPS, C), shape(8, C)),
        summed,
        chan,
        w_out_t,
    )
    return (
        late["input"],
        jnp.transpose(grad_kernel, (2, 0, 1)),
        vectors[3],
        vectors[1],
        vectors[2],
        h_sum,
        jnp.transpose(g_sum),
        vectors[4],
        vectors[5],
    )


def solution(mesh):
    split = P(None, "lat", "lon")
    return jax.shard_map(
        local,
        mesh=mesh,
        in_specs=(split,) * 7 + (P(),) * 8,
        out_specs=(split,) + (P(),) * 8,
        check_vma=False,
    )
```

```python
import functools
import math

import jax
import jax.numpy as jnp
from jax import lax
from jax.experimental import pallas as pl
from jax.experimental.pallas import tpu as pltpu
from jax.sharding import PartitionSpec as P

C = 192
FF = 768
WORDS = FF // 4
GROUP = 64
RADIUS = 3
TAPS = 2 * RADIUS + 1
ROWS = 4
COLS = 450
WIDE = COLS + 2 * RADIUS
LANES = 512
MAIN = 384
TAIL = COLS + RADIUS - MAIN
PACK = 1408
RIM = MAIN * RADIUS + TAIL * RADIUS - (PACK - 128)
CH = 16
F32 = jnp.float32
BF16 = jnp.bfloat16
VMEM_LIMIT = 18 * 1024 * 1024


def params():
    return pltpu.CompilerParams(vmem_limit_bytes=VMEM_LIMIT)


def resident(kernel, name, out_shape, *args, scratch=(), space=pltpu.VMEM, cost=0):
    spec = pl.BlockSpec(memory_space=pltpu.VMEM)
    return pl.pallas_call(
        kernel,
        out_shape=out_shape,
        in_specs=[pl.BlockSpec(memory_space=space)] * len(args),
        out_specs=jax.tree.map(lambda _: spec, out_shape),
        scratch_shapes=list(scratch),
        cost_estimate=pl.CostEstimate(flops=0, bytes_accessed=cost, transcendentals=0),
        compiler_params=params(),
        name=name,
    )(*args)


def lane_iota(shape):
    return lax.broadcasted_iota(jnp.int32, shape, len(shape) - 1)


def nt_dot(a, b):
    return lax.dot_general(a, b, (((1,), (1,)), ((), ())), preferred_element_type=F32)


def nn_dot(a, b):
    return jnp.dot(a, b, preferred_element_type=F32)


def rims_of(rows, head):
    first = RADIUS if head else COLS
    base = RIM + (RADIUS * ROWS if head else 0)
    lane = lane_iota((C, 128))
    total = jnp.zeros((C, 128), F32)
    for r, row in enumerate(rows):
        start = base + RADIUS * r
        moved = pltpu.roll(row, (start - first) % LANES, 1)[:, :128]
        keep = (lane >= start) & (lane < start + RADIUS)
        total = jnp.where(keep, moved, total)
    return total.astype(BF16)


def pack(rows, ref):
    lane = lane_iota((C, 256))
    tails = jnp.zeros((C, 256), F32)
    for k, value in enumerate(rows):
        ref[:, MAIN * k : MAIN * (k + 1)] = value[:, :MAIN].astype(BF16)
        wide = jnp.concatenate([value[:, MAIN:], jnp.zeros((C, 128), F32)], axis=1)
        moved = pltpu.roll(wide, TAIL * k, 1) if k else wide
        keep = (lane >= TAIL * k) & (lane < TAIL * (k + 1))
        tails = jnp.where(keep, moved, tails)
    ref[:, MAIN * RADIUS :] = tails.astype(BF16)


def send_rows(rows, head_ref, tail_ref, up_ref, down_ref):
    pack(rows[:RADIUS], up_ref)
    pack(rows[ROWS - RADIUS :], down_ref)
    head_ref[...] = rims_of(rows, True)
    tail_ref[...] = rims_of(rows, False)


def with_rims(first_tile, last_tile, rims, r):
    lane = lane_iota((C, 128))
    left = pltpu.roll(rims, (-RIM - RADIUS * r) % 128, 1)
    spot = RADIUS + COLS - MAIN
    right = pltpu.roll(rims, (spot - RIM - RADIUS * (ROWS + r)) % 128, 1)
    first_tile = jnp.where(lane < RADIUS, left, first_tile)
    last_tile = jnp.where((lane >= spot) & (lane < spot + RADIUS), right, last_tile)
    return first_tile.astype(BF16), last_tile.astype(BF16)


def fill_halo(field_ref, ref, first_row, source_row):
    rims = ref[:, PACK - 128 :].astype(F32)
    tails = ref[:, MAIN * RADIUS :].astype(F32)
    lane = lane_iota((C, 128))
    for k in range(RADIUS):
        moved = pltpu.roll(tails, (-TAIL * k) % 256, 1) if k else tails
        last = jnp.where(lane < TAIL, moved[:, :128], 0.0)
        first, last = with_rims(
            ref[:, MAIN * k : MAIN * k + 128].astype(F32), last, rims, source_row + k
        )
        field_ref[first_row + k, :, :128] = first
        field_ref[first_row + k, :, 128:MAIN] = ref[:, MAIN * k + 128 : MAIN * (k + 1)]
        field_ref[first_row + k, :, MAIN:] = last


def fetch(sources, targets, sems, meanwhile=None):
    copies = [
        pltpu.make_async_copy(source, target, sems.at[k])
        for k, (source, target) in enumerate(zip(sources, targets))
    ]
    for copy in copies:
        copy.start()
    if meanwhile is not None:
        meanwhile()
    for copy in copies:
        copy.wait()


def restore_kernel(
    words_hbm, low_hbm, high_hbm, own_ref, head_ref, tail_ref, up_ref, down_ref,
    words_ref, low_ref, high_ref, bounds, sems,
):
    fetch((words_hbm, low_hbm, high_hbm), (words_ref, low_ref, high_ref), sems)
    nwords = C // 4
    bounds[...] = jnp.zeros(bounds.shape, F32)
    for g in range(C // GROUP):
        low = low_ref[g].astype(F32)
        bounds[0, g, :, :COLS] = low
        bounds[1, g, :, :COLS] = high_ref[g].astype(F32) - low
    per = GROUP // 4
    row_id = lax.broadcasted_iota(jnp.int32, (C, C), 0)
    col_id = lax.broadcasted_iota(jnp.int32, (C, C), 1)
    place = (row_id == 4 * (col_id % nwords) + col_id // nwords).astype(F32).astype(BF16)
    lane = lane_iota((C, LANES))
    rows = []
    for r in range(ROWS):
        pieces = []
        words = words_ref[:, r, :]
        words = jnp.concatenate([words, jnp.zeros((nwords, LANES - COLS), jnp.int32)], axis=1)
        for j in range(4):
            code = (jnp.right_shift(words, 2 * j) & 3).astype(F32)
            for g in range(C // GROUP):
                low = bounds[0, g, r : r + 1, :]
                span = bounds[1, g, r : r + 1, :]
                value = low + code[g * per : (g + 1) * per] * span / 3.0
                pieces.append(value.astype(BF16))
        mixed = jnp.concatenate(pieces, axis=0)
        value = nn_dot(place, mixed)
        value = pltpu.roll(value, RADIUS, 1)
        value = jnp.where((lane >= RADIUS) & (lane < RADIUS + COLS), value, 0.0)
        rows.append(value)
        own_ref[r] = value.astype(BF16)
    send_rows(rows, head_ref, tail_ref, up_ref, down_ref)


def natural_order(order):
    row_id = lax.broadcasted_iota(jnp.int32, (FF, FF), 0)
    col_id = lax.broadcasted_iota(jnp.int32, (FF, FF), 1)
    order[...] = (col_id == 4 * (row_id % WORDS) + row_id // WORDS).astype(F32).astype(BF16)


def reorder(value, order):
    high = value.astype(BF16)
    rest = (value - high.astype(F32)).astype(BF16)
    return nn_dot(high, order[...]) + nn_dot(rest, order[...])


def mlp_kernel(
    words_hbm, low_hbm, high_hbm, grad_hbm, chan_hbm, w_out_hbm, w_in_hbm,
    hidden_ref, normed_ref, g_ref, sums_ref, rows_ref,
    words_ref, low_ref, high_ref, grad_ref, chan_ref, w_out_ref, w_in_ref, sems,
    order, w_out_p, w_in_p, lifted, active, bounds, grads,
):
    fetch(
        (w_out_hbm, w_in_hbm, low_hbm, high_hbm, grad_hbm, words_hbm, chan_hbm),
        (w_out_ref, w_in_ref, low_ref, high_ref, grad_ref, words_ref, chan_ref),
        sems,
        functools.partial(natural_order, order),
    )
    w_out_p[...] = nt_dot(order[...], w_out_ref[...]).astype(BF16)
    w_in_p[...] = nt_dot(w_in_ref[...], order[...]).astype(BF16)
    groups = FF // GROUP
    bounds[...] = jnp.zeros(bounds.shape, F32)
    grads[...] = grad_ref[...].astype(F32)
    for g in range(groups):
        low = low_ref[g].astype(F32)
        span = high_ref[g].astype(F32) - low
        for k in range(4):
            hidden = low + float(k) * span / 3.0
            cdf = 0.5 * (1.0 + lax.erf(hidden * 0.7071067811865476))
            density = jnp.exp(-0.5 * hidden * hidden) * 0.3989422804014327
            bounds[k, g, :, :COLS] = hidden * cdf
            bounds[4 + k, g, :, :COLS] = cdf + hidden * density
    g_sum = jnp.zeros((C, FF), F32)
    total = jnp.zeros((C, 1), F32)
    for r in range(ROWS):
        grad = grads[:, r, :]
        grad = jnp.concatenate([grad, jnp.zeros((C, LANES - COLS), F32)], axis=1)
        total = total + jnp.sum(grad, axis=1, keepdims=True)
        rows_ref[r] = grad.astype(BF16)
        scaled = (chan_ref[:, 3:4] * grad).astype(BF16)
        lifted[...] = nn_dot(w_out_p[...], scaled)
        words_row = words_ref[:, r, :]
        words_row = jnp.concatenate(
            [words_row, jnp.zeros((WORDS, LANES - COLS), jnp.int32)], axis=1
        )
        for g in range(groups):
            words = words_row[CH * g : CH * (g + 1)]
            values = [
                jnp.broadcast_to(bounds[k, g, r : r + 1, :], (CH, LANES)) for k in range(8)
            ]
            for j in range(4):
                odd = (words & (1 << (2 * j))) != 0
                upper = (words & (2 << (2 * j))) != 0
                act = jnp.where(
                    upper,
                    jnp.where(odd, values[3], values[2]),
                    jnp.where(odd, values[1], values[0]),
                )
                slope = jnp.where(
                    upper,
                    jnp.where(odd, values[7], values[6]),
                    jnp.where(odd, values[5], values[4]),
                )
                place = slice(WORDS * j + CH * g, WORDS * j + CH * (g + 1))
                active[place, :] = act.astype(BF16)
                hidden_ref[r, place, :] = (lifted[place, :] * slope).astype(BF16)
        normed_ref[r] = nn_dot(w_in_p[...], hidden_ref[r])
        g_sum = g_sum + nt_dot(rows_ref[r], active[...])
    sums_ref[...] = jnp.where(lane_iota((C, 128)) == 52, total, 0.0)
    g_ref[...] = reorder(g_sum, order)


OWN = tuple(range(RADIUS, RADIUS + ROWS))
HALO = tuple(range(RADIUS)) + tuple(range(RADIUS + ROWS, 2 * RADIUS + ROWS))


def stencil(cell, used, taps_ref, wide_taps, partial, emit, flip):
    def body(block, carry):
        chans = pl.ds(pl.multiple_of(block * CH, CH), CH)
        taps = taps_ref[chans, :]
        for t in range(TAPS * TAPS):
            source = TAPS * TAPS - 1 - t if flip else t
            wide_taps[t] = jnp.broadcast_to(taps[:, source : source + 1], (CH, 128))
        for tile in range(LANES // 128):
            lanes = slice(128 * tile, 128 * (tile + 1))
            cells = {r: cell(r, chans, lanes).astype(F32) for r in used}
            for q in range(TAPS):
                sums = [None] * ROWS
                for p in range(TAPS):
                    tap = wide_taps[TAPS * p + q]
                    for i in range(ROWS):
                        if i + p in cells:
                            term = tap * cells[i + p]
                            sums[i] = term if sums[i] is None else sums[i] + term
                for i in range(ROWS):
                    partial[q, i, :, lanes] = sums[i]
        for i in range(ROWS):
            total = partial[0, i]
            for q in range(1, TAPS):
                total = total + pltpu.roll(partial[q, i], LANES - q, 1)
            emit(chans, i, total)
        return carry

    lax.fori_loop(0, C // CH, body, 0)


def own_kernel(own_ref, rims_ref, taps_ref, filled_ref, total_ref, wide_taps, partial, *, flip):
    rims = rims_ref[...].astype(F32)
    for r in range(ROWS):
        first, last = with_rims(
            own_ref[r, :, :128].astype(F32), own_ref[r, :, MAIN:].astype(F32), rims, r
        )
        filled_ref[r, :, :128] = first
        filled_ref[r, :, 128:MAIN] = own_ref[r, :, 128:MAIN]
        filled_ref[r, :, MAIN:] = last

    def emit(chans, i, total):
        total_ref[i, chans, :] = total

    def cell(r, chans, lanes):
        return filled_ref[r - RADIUS, chans, lanes]

    stencil(cell, OWN, taps_ref, wide_taps, partial, emit, flip)


def conv_kernel(
    filled_ref, total_ref, above_ref, below_ref, taps_ref, chan_ref, normed_ref,
    field_ref, grad_ref, head_ref, tail_ref, up_ref, down_ref, normed_in_ref, sums_ref,
    conv, sums, wide_taps, partial,
):
    fill_halo(field_ref, above_ref, 0, ROWS - RADIUS)
    fill_halo(field_ref, below_ref, RADIUS + ROWS, 0)
    field_ref[RADIUS : RADIUS + ROWS] = filled_ref[...]

    def emit(chans, i, total):
        conv[i, chans, :] = total_ref[i, chans, :] + (total + chan_ref[chans, 0:1])

    def cell(r, chans, lanes):
        return field_ref[r, chans, lanes]

    stencil(cell, HALO, taps_ref, wide_taps, partial, emit, False)
    gain = jnp.broadcast_to(chan_ref[:, 1:2], (C, 128))
    bias = jnp.broadcast_to(chan_ref[:, 2:3], (C, 128))
    sums[...] = jnp.zeros(sums.shape, F32)
    rows = []
    for r in range(ROWS):
        for tile in range(LANES // 128):
            lanes = slice(128 * tile, 128 * (tile + 1))
            value = conv[r, :, lanes]
            centered = value - jnp.sum(value, axis=0, keepdims=True) * (1.0 / C)
            variance = jnp.sum(centered * centered, axis=0, keepdims=True) * (1.0 / C)
            inv_std = lax.rsqrt(variance + 1e-06)
            normed = centered * inv_std
            normed_in_ref[r, :, lanes] = (normed * gain + bias).astype(BF16)
            back = normed_ref[r, :, lanes]
            sums[0] += back * normed
            sums[1] += back
            dn = back * gain
            mean_dn = jnp.sum(dn, axis=0, keepdims=True) * (1.0 / C)
            mean_dx = jnp.sum(dn * normed, axis=0, keepdims=True) * (1.0 / C)
            grad = inv_std * (dn - mean_dn - normed * mean_dx)
            if 128 * (tile + 1) > COLS:
                grad = jnp.where(lane_iota((C, 128)) < COLS - 128 * tile, grad, 0.0)
            grad = grad.astype(BF16).astype(F32)
            sums[2] += grad
            conv[r, :, lanes] = grad
        grad = pltpu.roll(conv[r], RADIUS, 1)
        rows.append(grad)
        grad_ref[r] = grad.astype(BF16)
    send_rows(rows, head_ref, tail_ref, up_ref, down_ref)
    lane = lane_iota((C, 128))
    total = jnp.zeros((C, 128), F32)
    for k in range(3):
        total = jnp.where(lane == 49 + k, jnp.sum(sums[k], axis=1, keepdims=True), total)
    sums_ref[...] = total


def weight_kernel(normed_in_ref, hidden_ref, h_ref, order):
    natural_order(order)
    h_sum = jnp.zeros((C, FF), F32)
    for r in range(ROWS):
        h_sum = h_sum + nt_dot(normed_in_ref[r], hidden_ref[r])
    h_ref[...] = reorder(h_sum, order)


def taps_kernel(field_ref, grad_ref, sums_ref):
    row = lax.broadcasted_iota(jnp.int32, (CH, 256), 0)
    diagonal = lane_iota((CH, 256)) % CH == row
    row = lax.broadcasted_iota(jnp.int32, (128, 128), 0)
    pick = (TAPS * (row // CH) == lane_iota((128, 128))).astype(F32).astype(BF16)
    cells = (ROWS + 2 * RADIUS) * CH
    lane = lane_iota((CH, 128))

    def body(block, carry):
        chans = pl.ds(pl.multiple_of(block * CH, CH), CH)
        field = field_ref[:, chans, :].reshape(cells, LANES)
        grads = [grad_ref[i, chans, :] for i in range(ROWS)]
        moved = [
            pltpu.roll(grads[i], (q - RADIUS) % LANES, 1) if q != RADIUS else grads[i]
            for q in range(TAPS)
            for i in range(ROWS)
        ]
        product = nt_dot(jnp.concatenate(moved, axis=0), field)
        product = jnp.concatenate(
            [product, jnp.zeros((TAPS * ROWS * CH, 256 - cells), F32)], axis=1
        )
        totals = []
        for q in range(TAPS):
            total = None
            for i in range(ROWS):
                start = (q * ROWS + i) * CH
                value = jnp.where(diagonal, product[start : start + CH], 0.0)
                value = (pltpu.roll(value, 256 - CH * i, 1) if i else value)[:, :128]
                total = value if total is None else total + value
            totals.append(jnp.where(lane < TAPS * CH, total, 0.0))
        total = jnp.concatenate(totals, axis=0)
        high = total.astype(BF16)
        rest = (total - high.astype(F32)).astype(BF16)
        result = nn_dot(high, pick) + nn_dot(rest, pick)
        sums = jnp.zeros((CH, 128), F32)
        for q in range(TAPS):
            value = result[q * CH : (q + 1) * CH]
            value = pltpu.roll(value, q, 1) if q else value
            sums = jnp.where(lane % TAPS == q, value, sums)
        sums = jnp.where(lane < TAPS * TAPS, sums, 0.0)
        sums_ref[chans, :] = sums
        return carry

    lax.fori_loop(0, C // CH, body, 0, unroll=2)


def halo_kernel(above_ref, below_ref, field_ref):
    fill_halo(field_ref, above_ref, 0, ROWS - RADIUS)
    fill_halo(field_ref, below_ref, RADIUS, 0)


def input_kernel(total_ref, field, taps_ref, grad_ref, out_ref, wide_taps, partial):

    def emit(chans, i, total):
        total = total + total_ref[i, chans, :]
        out_ref[i, chans, :] = (grad_ref[i, chans, :].astype(F32) + total).astype(BF16)

    def cell(r, chans, lanes):
        return field[r if r < RADIUS else r - ROWS, chans, lanes]

    stencil(cell, HALO, taps_ref, wide_taps, partial, emit, True)


def final_kernel(total_ref, extra_ref, chan_ref, w_out_ref, g_ref, h_ref, taps_ref, vectors_ref, *, factor):
    g_sum = total_ref[:, :FF].astype(F32) * factor
    h_ref[...] = total_ref[:, FF : 2 * FF].astype(F32) * factor
    sums = (total_ref[:, 2 * FF :].astype(F32) + extra_ref[...]) * factor
    scale = chan_ref[:, 3:4]
    g_ref[...] = g_sum * scale
    total = jnp.sum(g_sum * w_out_ref[...].astype(F32), axis=1, keepdims=True)
    sum_grad = sums[:, 52:53]
    lane = lane_iota((C, 128))
    sums = jnp.where(lane == 53, total + chan_ref[:, 4:5] * sum_grad, sums)
    sums = jnp.where(lane == 52, sum_grad * scale, sums)
    flat = jnp.transpose(sums)
    for p in range(TAPS):
        taps_ref[p] = flat[TAPS * p : TAPS * (p + 1)]
    vectors_ref[...] = flat[48:56]


def ring(axis, count):
    ahead = [(i, (i + 1) % count) for i in range(count)]
    return functools.partial(lax.ppermute, axis_name=axis, perm=ahead), functools.partial(
        lax.ppermute, axis_name=axis, perm=[(b, a) for a, b in ahead]
    )


def add_rims(head, tail, up, down):
    ahead, behind = ring("lon", lax.axis_size("lon"))
    rims = ahead(tail) + behind(head)
    up = jnp.concatenate([up[:, : PACK - 128], up[:, PACK - 128 :] + rims], axis=1)
    down = jnp.concatenate([down[:, : PACK - 128], down[:, PACK - 128 :] + rims], axis=1)
    return rims, up, down


def lat_rows(up, down):
    count = lax.axis_size("lat")
    above = lax.ppermute(down, "lat", [(i, i + 1) for i in range(count - 1)])
    below = lax.ppermute(up, "lat", [(i + 1, i) for i in range(count - 1)])
    return above, below


def swap(value, bits):
    count = lax.axis_size("lat") * lax.axis_size("lon")
    return lax.ppermute(value, ("lat", "lon"), [(i, i ^ bits) for i in range(count)])


def rounded(value):
    return lax.reduce_precision(value, 8, 7)


def by_index(index, parts):
    low = jnp.where((index & 1) != 0, parts[1], parts[0])
    high = jnp.where((index & 1) != 0, parts[3], parts[2])
    return jnp.where((index & 2) != 0, high, low)


def halved(value):
    core = lax.axis_index("lon") & 1
    half = value.shape[0] // 2
    low, high = value[:half], value[half:]
    sent = jnp.where(core != 0, low, high)
    return jnp.where(core != 0, high, low) + swap(sent, 1)


def all_sum(value, hooks):
    me = lax.axis_index("lat") * lax.axis_size("lon") + lax.axis_index("lon")
    core, z = me & 1, (me >> 2) & 3
    value = hooks(1, halved(hooks(0, value)))
    size = value.shape[0] // 4
    quarters = [value[size * k : size * (k + 1)] for k in range(4)]
    total = by_index(z, quarters)
    for k in range(1, 4):
        total = total + swap(by_index(z ^ k, quarters).astype(BF16), 4 * k).astype(F32)
    value = total
    step = 2
    for first, second in ((32, 64), (2, 16)):
        value = hooks(step, value)
        step += 1
        mine = rounded(value)
        sent = mine.astype(BF16)
        near, far, both = (swap(sent, b).astype(F32) for b in (first, second, first | second))
        value = (mine + near) + (far + both)
    value = hooks(4, rounded(value).astype(BF16))
    parts = [value] + [swap(value, 4 * k) for k in range(1, 4)]
    value = jnp.concatenate([by_index(z ^ k, parts) for k in range(4)], axis=0)
    value = hooks(5, value)
    other = swap(value, 1)
    width = value.shape[1] - 256
    taps = value[:, width:].astype(F32) + other[:, width:].astype(F32)
    taps = taps.reshape(4, C // 8, 2, 128)
    taps = jnp.transpose(taps, (0, 2, 1, 3)).reshape(C, 128)
    value, other = value[:, :width], other[:, :width]
    low, high = jnp.where(core != 0, other, value), jnp.where(core != 0, value, other)
    return jnp.concatenate([low, high], axis=0), taps


def local(
    stash_input, input_low, input_high, stash_hidden, hidden_low, hidden_high, grad_out,
    kernel, conv_bias, norm_gain, norm_bias, w_in, w_out, out_bias, layer_scale,
):
    tie = lax.optimization_barrier

    def shape(*dims, dtype=F32):
        return jax.ShapeDtypeStruct(dims, dtype)

    field_shape = shape(ROWS, C, LANES, dtype=BF16)
    total_shape = shape(ROWS, C, LANES)
    rim_shape = shape(C, 128, dtype=BF16)
    pack_shape = shape(C, PACK, dtype=BF16)
    sums_shape = shape(C, 128)
    weight_shape = shape(C, FF)
    own, head, tail, up, down = resident(
        restore_kernel,
        "restore",
        (field_shape, rim_shape, rim_shape, pack_shape, pack_shape),
        stash_input,
        input_low,
        input_high,
        scratch=[
            pltpu.VMEM(stash_input.shape, jnp.int32),
            pltpu.VMEM(input_low.shape, BF16),
            pltpu.VMEM(input_high.shape, BF16),
            pltpu.VMEM((2, C // GROUP, ROWS, LANES), F32),
            pltpu.SemaphoreType.DMA((3,)),
        ],
        space=pltpu.HBM,
    )
    rims, up, down = add_rims(head, tail, up, down)
    above, below = lat_rows(up, down)

    taps = jnp.pad(kernel.reshape(C, TAPS * TAPS), ((0, 0), (0, 128 - TAPS * TAPS)))
    chan = jnp.stack([conv_bias, norm_gain, norm_bias, layer_scale, out_bias], axis=1)
    chan = jnp.pad(chan, ((0, 0), (0, 123)))
    w_out_t = jnp.transpose(w_out)
    stencil_scratch = [
        pltpu.VMEM((TAPS * TAPS, CH, 128), F32),
        pltpu.VMEM((TAPS, ROWS, CH, LANES), F32),
    ]
    hidden_back, normed_back, g_part, sums_a, grad_rows = resident(
        mlp_kernel,
        "mlp",
        (
            shape(ROWS, FF, LANES, dtype=BF16),
            total_shape,
            weight_shape,
            sums_shape,
            field_shape,
        ),
        stash_hidden,
        hidden_low,
        hidden_high,
        grad_out,
        chan,
        w_out_t,
        w_in,
        space=pltpu.HBM,
        scratch=[
            pltpu.VMEM(stash_hidden.shape, jnp.int32),
            pltpu.VMEM(hidden_low.shape, BF16),
            pltpu.VMEM(hidden_high.shape, BF16),
            pltpu.VMEM(grad_out.shape, BF16),
            pltpu.VMEM(chan.shape, F32),
            pltpu.VMEM((C, FF), BF16),
            pltpu.VMEM((C, FF), BF16),
            pltpu.SemaphoreType.DMA((7,)),
            pltpu.VMEM((FF, FF), BF16),
            pltpu.VMEM((FF, C), BF16),
            pltpu.VMEM((C, FF), BF16),
            pltpu.VMEM((FF, LANES), F32),
            pltpu.VMEM((FF, LANES), BF16),
            pltpu.VMEM((8, FF // GROUP, ROWS, LANES), F32),
            pltpu.VMEM(grad_out.shape, F32),
        ],
    )

    def over_own(own, rims, flip, name):
        return resident(
            functools.partial(own_kernel, flip=flip),
            name,
            (field_shape, total_shape),
            own,
            rims,
            taps,
            scratch=stencil_scratch,
        )

    filled, total = over_own(own, rims, False, "conv_own")
    field, grad_own, head, tail, up, down, normed_in, sums_b = resident(
        conv_kernel,
        "conv",
        (
            shape(ROWS + 2 * RADIUS, C, LANES, dtype=BF16),
            field_shape,
            rim_shape,
            rim_shape,
            pack_shape,
            pack_shape,
            field_shape,
            sums_shape,
        ),
        filled,
        total,
        above,
        below,
        taps,
        chan,
        normed_back,
        scratch=[pltpu.VMEM((ROWS, C, LANES), F32), pltpu.VMEM((3, C, 128), F32)]
        + stencil_scratch,
    )

    h_part = resident(
        weight_kernel,
        "weight",
        weight_shape,
        normed_in,
        hidden_back,
        scratch=[pltpu.VMEM((FF, FF), BF16)],
    )
    rims, up, down = add_rims(head, tail, up, down)
    above, below = lat_rows(up, down)
    late = {"own": grad_own, "above": above, "below": below}

    def hooks(step, value):
        if step == 1:
            value, late["grad"], _ = tie((value, grad_own, up))
            late["taps"] = resident(taps_kernel, "taps", sums_shape, field, late["grad"])
            parts = late["taps"].reshape(4, 2, C // 8, 128)
            parts = [parts[:, k].reshape(C // 2, 128) for k in range(2)]
            value = jnp.concatenate([value, *parts], axis=1)
            value, late["own"] = tie((value, late["own"]))
            late["total"] = over_own(late["own"], rims, True, "input_own")[1]
        elif step == 2:
            above, below, late["total"] = tie((late["above"], late["below"], late["total"]))
            halo = resident(
                halo_kernel,
                "halo",
                shape(2 * RADIUS, C, LANES, dtype=BF16),
                above,
                below,
                cost=0,
            )
            value, late["total"], late["halo"] = tie((value, late["total"], halo))
        elif step == 3:
            value, late["total"] = tie((value, late["total"]))
            late["input"] = resident(
                input_kernel,
                "input",
                field_shape,
                late["total"],
                late["halo"],
                taps,
                grad_rows,
                scratch=stencil_scratch,
            )
        elif step == 4:
            value, late["input"] = tie((value, late["input"]))
            late["input"] = jnp.transpose(late["input"][:, :, :COLS], (1, 0, 2))
        elif step == 5:
            value, late["input"] = tie((value, late["input"]))
        return value

    summed, summed_taps = all_sum(jnp.concatenate([g_part, h_part, sums_a + sums_b], axis=1), hooks)
    cells = ROWS * lax.axis_size("lat") * COLS * lax.axis_size("lon")
    g_sum, h_sum, grad_kernel, vectors = resident(
        functools.partial(final_kernel, factor=1.0 / math.sqrt(cells)),
        "final",
        (weight_shape, weight_shape, shape(TAPS, TAPS, C), shape(8, C)),
        summed,
        summed_taps,
        chan,
        w_out_t,
    )
    return (
        late["input"],
        jnp.transpose(grad_kernel, (2, 0, 1)),
        vectors[3],
        vectors[1],
        vectors[2],
        h_sum,
        jnp.transpose(g_sum),
        vectors[4],
        vectors[5],
    )


def solution(mesh):
    split = P(None, "lat", "lon")
    return jax.shard_map(
        local,
        mesh=mesh,
        in_specs=(split,) * 7 + (P(),) * 8,
        out_specs=(split,) + (P(),) * 8,
        check_vma=False,
    )
```

```python
import functools
import math

import jax
import jax.numpy as jnp
from jax import lax
from jax.experimental import pallas as pl
from jax.experimental.pallas import tpu as pltpu
from jax.sharding import PartitionSpec as P

C = 192
FF = 768
WORDS = FF // 4
GROUP = 64
RADIUS = 3
TAPS = 2 * RADIUS + 1
ROWS = 4
COLS = 450
WIDE = COLS + 2 * RADIUS
LANES = 512
MAIN = 384
TAIL = COLS + RADIUS - MAIN
PACK = 1408
RIM = MAIN * RADIUS + TAIL * RADIUS - (PACK - 128)
CH = 16
F32 = jnp.float32
BF16 = jnp.bfloat16
VMEM_LIMIT = 18 * 1024 * 1024


def params():
    return pltpu.CompilerParams(vmem_limit_bytes=VMEM_LIMIT)


def resident(kernel, name, out_shape, *args, scratch=(), space=pltpu.VMEM, cost=0):
    spec = pl.BlockSpec(memory_space=pltpu.VMEM)
    return pl.pallas_call(
        kernel,
        out_shape=out_shape,
        in_specs=[pl.BlockSpec(memory_space=space)] * len(args),
        out_specs=jax.tree.map(lambda _: spec, out_shape),
        scratch_shapes=list(scratch),
        cost_estimate=pl.CostEstimate(flops=0, bytes_accessed=cost, transcendentals=0),
        compiler_params=params(),
        name=name,
    )(*args)


def lane_iota(shape):
    return lax.broadcasted_iota(jnp.int32, shape, len(shape) - 1)


def nt_dot(a, b):
    return lax.dot_general(a, b, (((1,), (1,)), ((), ())), preferred_element_type=F32)


def nn_dot(a, b):
    return jnp.dot(a, b, preferred_element_type=F32)


def rims_of(rows, head):
    first = RADIUS if head else COLS
    base = RIM + (RADIUS * ROWS if head else 0)
    lane = lane_iota((C, 128))
    total = jnp.zeros((C, 128), F32)
    for r, row in enumerate(rows):
        start = base + RADIUS * r
        moved = pltpu.roll(row, (start - first) % LANES, 1)[:, :128]
        keep = (lane >= start) & (lane < start + RADIUS)
        total = jnp.where(keep, moved, total)
    return total.astype(BF16)


def pack(rows, ref):
    lane = lane_iota((C, 256))
    tails = jnp.zeros((C, 256), F32)
    for k, value in enumerate(rows):
        ref[:, MAIN * k : MAIN * (k + 1)] = value[:, :MAIN].astype(BF16)
        wide = jnp.concatenate([value[:, MAIN:], jnp.zeros((C, 128), F32)], axis=1)
        moved = pltpu.roll(wide, TAIL * k, 1) if k else wide
        keep = (lane >= TAIL * k) & (lane < TAIL * (k + 1))
        tails = jnp.where(keep, moved, tails)
    ref[:, MAIN * RADIUS :] = tails.astype(BF16)


def send_rows(rows, head_ref, tail_ref, up_ref, down_ref):
    pack(rows[:RADIUS], up_ref)
    pack(rows[ROWS - RADIUS :], down_ref)
    head_ref[...] = rims_of(rows, True)
    tail_ref[...] = rims_of(rows, False)


def with_rims(first_tile, last_tile, rims, r):
    lane = lane_iota((C, 128))
    left = pltpu.roll(rims, (-RIM - RADIUS * r) % 128, 1)
    spot = RADIUS + COLS - MAIN
    right = pltpu.roll(rims, (spot - RIM - RADIUS * (ROWS + r)) % 128, 1)
    first_tile = jnp.where(lane < RADIUS, left, first_tile)
    last_tile = jnp.where((lane >= spot) & (lane < spot + RADIUS), right, last_tile)
    return first_tile.astype(BF16), last_tile.astype(BF16)


def fill_halo(field_ref, ref, first_row, source_row):
    rims = ref[:, PACK - 128 :].astype(F32)
    tails = ref[:, MAIN * RADIUS :].astype(F32)
    lane = lane_iota((C, 128))
    for k in range(RADIUS):
        moved = pltpu.roll(tails, (-TAIL * k) % 256, 1) if k else tails
        last = jnp.where(lane < TAIL, moved[:, :128], 0.0)
        first, last = with_rims(
            ref[:, MAIN * k : MAIN * k + 128].astype(F32), last, rims, source_row + k
        )
        field_ref[first_row + k, :, :128] = first
        field_ref[first_row + k, :, 128:MAIN] = ref[:, MAIN * k + 128 : MAIN * (k + 1)]
        field_ref[first_row + k, :, MAIN:] = last


def fetch(sources, targets, sems, meanwhile=None):
    copies = [
        pltpu.make_async_copy(source, target, sems.at[k])
        for k, (source, target) in enumerate(zip(sources, targets))
    ]
    for copy in copies:
        copy.start()
    if meanwhile is not None:
        meanwhile()
    for copy in copies:
        copy.wait()


def restore_kernel(
    words_hbm, low_hbm, high_hbm, own_ref, head_ref, tail_ref, up_ref, down_ref,
    words_ref, low_ref, high_ref, bounds, sems,
):
    fetch((words_hbm, low_hbm, high_hbm), (words_ref, low_ref, high_ref), sems)
    nwords = C // 4
    bounds[...] = jnp.zeros(bounds.shape, F32)
    for g in range(C // GROUP):
        low = low_ref[g].astype(F32)
        bounds[0, g, :, :COLS] = low
        bounds[1, g, :, :COLS] = high_ref[g].astype(F32) - low
    per = GROUP // 4
    row_id = lax.broadcasted_iota(jnp.int32, (C, C), 0)
    col_id = lax.broadcasted_iota(jnp.int32, (C, C), 1)
    place = (row_id == 4 * (col_id % nwords) + col_id // nwords).astype(F32).astype(BF16)
    lane = lane_iota((C, LANES))
    rows = []
    for r in range(ROWS):
        pieces = []
        words = words_ref[:, r, :]
        words = jnp.concatenate([words, jnp.zeros((nwords, LANES - COLS), jnp.int32)], axis=1)
        for j in range(4):
            code = (jnp.right_shift(words, 2 * j) & 3).astype(F32)
            for g in range(C // GROUP):
                low = bounds[0, g, r : r + 1, :]
                span = bounds[1, g, r : r + 1, :]
                value = low + code[g * per : (g + 1) * per] * span / 3.0
                pieces.append(value.astype(BF16))
        mixed = jnp.concatenate(pieces, axis=0)
        value = nn_dot(place, mixed)
        value = pltpu.roll(value, RADIUS, 1)
        value = jnp.where((lane >= RADIUS) & (lane < RADIUS + COLS), value, 0.0)
        rows.append(value)
        own_ref[r] = value.astype(BF16)
    send_rows(rows, head_ref, tail_ref, up_ref, down_ref)


def natural_order(order):
    row_id = lax.broadcasted_iota(jnp.int32, (FF, FF), 0)
    col_id = lax.broadcasted_iota(jnp.int32, (FF, FF), 1)
    order[...] = (col_id == 4 * (row_id % WORDS) + row_id // WORDS).astype(F32).astype(BF16)


def reorder(value, order):
    high = value.astype(BF16)
    rest = (value - high.astype(F32)).astype(BF16)
    return nn_dot(high, order[...]) + nn_dot(rest, order[...])


def mlp_kernel(
    words_hbm, low_hbm, high_hbm, grad_hbm, chan_hbm, w_out_hbm, w_in_hbm,
    hidden_ref, normed_ref, g_ref, sums_ref, rows_ref,
    words_ref, low_ref, high_ref, grad_ref, chan_ref, w_out_ref, w_in_ref, sems,
    order, w_out_p, w_in_p, lifted, active, bounds, grads,
):
    fetch(
        (w_out_hbm, w_in_hbm, low_hbm, high_hbm, grad_hbm, words_hbm, chan_hbm),
        (w_out_ref, w_in_ref, low_ref, high_ref, grad_ref, words_ref, chan_ref),
        sems,
        functools.partial(natural_order, order),
    )
    w_out_p[...] = nt_dot(order[...], w_out_ref[...]).astype(BF16)
    w_in_p[...] = nt_dot(w_in_ref[...], order[...]).astype(BF16)
    groups = FF // GROUP
    bounds[...] = jnp.zeros(bounds.shape, F32)
    grads[...] = grad_ref[...].astype(F32)
    for g in range(groups):
        low = low_ref[g].astype(F32)
        span = high_ref[g].astype(F32) - low
        for k in range(4):
            hidden = low + float(k) * span / 3.0
            cdf = 0.5 * (1.0 + lax.erf(hidden * 0.7071067811865476))
            density = jnp.exp(-0.5 * hidden * hidden) * 0.3989422804014327
            bounds[k, g, :, :COLS] = hidden * cdf
            bounds[4 + k, g, :, :COLS] = cdf + hidden * density
    g_sum = jnp.zeros((C, FF), F32)
    total = jnp.zeros((C, 1), F32)
    for r in range(ROWS):
        grad = grads[:, r, :]
        grad = jnp.concatenate([grad, jnp.zeros((C, LANES - COLS), F32)], axis=1)
        total = total + jnp.sum(grad, axis=1, keepdims=True)
        rows_ref[r] = grad.astype(BF16)
        scaled = (chan_ref[:, 3:4] * grad).astype(BF16)
        lifted[...] = nn_dot(w_out_p[...], scaled)
        words_row = words_ref[:, r, :]
        words_row = jnp.concatenate(
            [words_row, jnp.zeros((WORDS, LANES - COLS), jnp.int32)], axis=1
        )
        for g in range(groups):
            words = words_row[CH * g : CH * (g + 1)]
            values = [
                jnp.broadcast_to(bounds[k, g, r : r + 1, :], (CH, LANES)) for k in range(8)
            ]
            for j in range(4):
                odd = (words & (1 << (2 * j))) != 0
                upper = (words & (2 << (2 * j))) != 0
                act = jnp.where(
                    upper,
                    jnp.where(odd, values[3], values[2]),
                    jnp.where(odd, values[1], values[0]),
                )
                slope = jnp.where(
                    upper,
                    jnp.where(odd, values[7], values[6]),
                    jnp.where(odd, values[5], values[4]),
                )
                place = slice(WORDS * j + CH * g, WORDS * j + CH * (g + 1))
                active[place, :] = act.astype(BF16)
                hidden_ref[r, place, :] = (lifted[place, :] * slope).astype(BF16)
        normed_ref[r] = nn_dot(w_in_p[...], hidden_ref[r])
        g_sum = g_sum + nt_dot(rows_ref[r], active[...])
    sums_ref[...] = jnp.where(lane_iota((C, 128)) == 52, total, 0.0)
    g_ref[...] = reorder(g_sum, order)


OWN = tuple(range(RADIUS, RADIUS + ROWS))
HALO = tuple(range(RADIUS)) + tuple(range(RADIUS + ROWS, 2 * RADIUS + ROWS))


def stencil(cell, used, taps_ref, wide_taps, partial, emit, flip):
    def body(block, carry):
        chans = pl.ds(pl.multiple_of(block * CH, CH), CH)
        taps = taps_ref[chans, :]
        for t in range(TAPS * TAPS):
            source = TAPS * TAPS - 1 - t if flip else t
            wide_taps[t] = jnp.broadcast_to(taps[:, source : source + 1], (CH, 128))
        for tile in range(LANES // 128):
            lanes = slice(128 * tile, 128 * (tile + 1))
            cells = {r: cell(r, chans, lanes).astype(F32) for r in used}
            for q in range(TAPS):
                sums = [None] * ROWS
                for p in range(TAPS):
                    tap = wide_taps[TAPS * p + q]
                    for i in range(ROWS):
                        if i + p in cells:
                            term = tap * cells[i + p]
                            sums[i] = term if sums[i] is None else sums[i] + term
                for i in range(ROWS):
                    partial[q, i, :, lanes] = sums[i]
        for i in range(ROWS):
            total = partial[0, i]
            for q in range(1, TAPS):
                total = total + pltpu.roll(partial[q, i], LANES - q, 1)
            emit(chans, i, total)
        return carry

    lax.fori_loop(0, C // CH, body, 0, unroll=2)


def own_kernel(own_ref, rims_ref, taps_ref, filled_ref, total_ref, wide_taps, partial, *, flip):
    rims = rims_ref[...].astype(F32)
    for r in range(ROWS):
        first, last = with_rims(
            own_ref[r, :, :128].astype(F32), own_ref[r, :, MAIN:].astype(F32), rims, r
        )
        filled_ref[r, :, :128] = first
        filled_ref[r, :, 128:MAIN] = own_ref[r, :, 128:MAIN]
        filled_ref[r, :, MAIN:] = last

    def emit(chans, i, total):
        total_ref[i, chans, :] = total

    def cell(r, chans, lanes):
        return filled_ref[r - RADIUS, chans, lanes]

    stencil(cell, OWN, taps_ref, wide_taps, partial, emit, flip)


def conv_kernel(
    filled_ref, total_ref, above_ref, below_ref, taps_ref, chan_ref, normed_ref,
    field_ref, grad_ref, head_ref, tail_ref, up_ref, down_ref, normed_in_ref, sums_ref,
    conv, sums, wide_taps, partial,
):
    fill_halo(field_ref, above_ref, 0, ROWS - RADIUS)
    fill_halo(field_ref, below_ref, RADIUS + ROWS, 0)
    field_ref[RADIUS : RADIUS + ROWS] = filled_ref[...]

    def emit(chans, i, total):
        conv[i, chans, :] = total_ref[i, chans, :] + (total + chan_ref[chans, 0:1])

    def cell(r, chans, lanes):
        return field_ref[r, chans, lanes]

    stencil(cell, HALO, taps_ref, wide_taps, partial, emit, False)
    gain = jnp.broadcast_to(chan_ref[:, 1:2], (C, 128))
    bias = jnp.broadcast_to(chan_ref[:, 2:3], (C, 128))
    sums[...] = jnp.zeros(sums.shape, F32)
    rows = []
    for r in range(ROWS):
        for tile in range(LANES // 128):
            lanes = slice(128 * tile, 128 * (tile + 1))
            value = conv[r, :, lanes]
            centered = value - jnp.sum(value, axis=0, keepdims=True) * (1.0 / C)
            variance = jnp.sum(centered * centered, axis=0, keepdims=True) * (1.0 / C)
            inv_std = lax.rsqrt(variance + 1e-06)
            normed = centered * inv_std
            normed_in_ref[r, :, lanes] = (normed * gain + bias).astype(BF16)
            back = normed_ref[r, :, lanes]
            sums[0] += back * normed
            sums[1] += back
            dn = back * gain
            mean_dn = jnp.sum(dn, axis=0, keepdims=True) * (1.0 / C)
            mean_dx = jnp.sum(dn * normed, axis=0, keepdims=True) * (1.0 / C)
            grad = inv_std * (dn - mean_dn - normed * mean_dx)
            if 128 * (tile + 1) > COLS:
                grad = jnp.where(lane_iota((C, 128)) < COLS - 128 * tile, grad, 0.0)
            grad = grad.astype(BF16).astype(F32)
            sums[2] += grad
            conv[r, :, lanes] = grad
        grad = pltpu.roll(conv[r], RADIUS, 1)
        rows.append(grad)
        grad_ref[r] = grad.astype(BF16)
    send_rows(rows, head_ref, tail_ref, up_ref, down_ref)
    lane = lane_iota((C, 128))
    total = jnp.zeros((C, 128), F32)
    for k in range(3):
        total = jnp.where(lane == 49 + k, jnp.sum(sums[k], axis=1, keepdims=True), total)
    sums_ref[...] = total


def weight_kernel(normed_in_ref, hidden_ref, h_ref, order):
    natural_order(order)
    h_sum = jnp.zeros((C, FF), F32)
    for r in range(ROWS):
        h_sum = h_sum + nt_dot(normed_in_ref[r], hidden_ref[r])
    h_ref[...] = reorder(h_sum, order)


def taps_kernel(field_ref, grad_ref, sums_ref):
    row = lax.broadcasted_iota(jnp.int32, (CH, 256), 0)
    diagonal = lane_iota((CH, 256)) % CH == row
    row = lax.broadcasted_iota(jnp.int32, (128, 128), 0)
    pick = (TAPS * (row // CH) == lane_iota((128, 128))).astype(F32).astype(BF16)
    cells = (ROWS + 2 * RADIUS) * CH
    lane = lane_iota((CH, 128))

    def body(block, carry):
        chans = pl.ds(pl.multiple_of(block * CH, CH), CH)
        field = field_ref[:, chans, :].reshape(cells, LANES)
        grads = [grad_ref[i, chans, :] for i in range(ROWS)]
        moved = [
            pltpu.roll(grads[i], (q - RADIUS) % LANES, 1) if q != RADIUS else grads[i]
            for q in range(TAPS)
            for i in range(ROWS)
        ]
        product = nt_dot(jnp.concatenate(moved, axis=0), field)
        product = jnp.concatenate(
            [product, jnp.zeros((TAPS * ROWS * CH, 256 - cells), F32)], axis=1
        )
        totals = []
        for q in range(TAPS):
            total = None
            for i in range(ROWS):
                start = (q * ROWS + i) * CH
                value = jnp.where(diagonal, product[start : start + CH], 0.0)
                value = (pltpu.roll(value, 256 - CH * i, 1) if i else value)[:, :128]
                total = value if total is None else total + value
            totals.append(jnp.where(lane < TAPS * CH, total, 0.0))
        total = jnp.concatenate(totals, axis=0)
        high = total.astype(BF16)
        rest = (total - high.astype(F32)).astype(BF16)
        result = nn_dot(high, pick) + nn_dot(rest, pick)
        sums = jnp.zeros((CH, 128), F32)
        for q in range(TAPS):
            value = result[q * CH : (q + 1) * CH]
            value = pltpu.roll(value, q, 1) if q else value
            sums = jnp.where(lane % TAPS == q, value, sums)
        sums = jnp.where(lane < TAPS * TAPS, sums, 0.0)
        sums_ref[chans, :] = sums
        return carry

    lax.fori_loop(0, C // CH, body, 0, unroll=4)


def halo_kernel(above_ref, below_ref, field_ref):
    fill_halo(field_ref, above_ref, 0, ROWS - RADIUS)
    fill_halo(field_ref, below_ref, RADIUS, 0)


def input_kernel(total_ref, field, taps_ref, grad_ref, out_ref, wide_taps, partial):

    def emit(chans, i, total):
        total = total + total_ref[i, chans, :]
        out_ref[i, chans, :] = (grad_ref[i, chans, :].astype(F32) + total).astype(BF16)

    def cell(r, chans, lanes):
        return field[r if r < RADIUS else r - ROWS, chans, lanes]

    stencil(cell, HALO, taps_ref, wide_taps, partial, emit, True)


def final_kernel(total_ref, extra_ref, chan_ref, w_out_ref, g_ref, h_ref, taps_ref, vectors_ref, *, factor):
    g_sum = total_ref[:, :FF].astype(F32) * factor
    h_ref[...] = total_ref[:, FF : 2 * FF].astype(F32) * factor
    sums = (total_ref[:, 2 * FF :].astype(F32) + extra_ref[...]) * factor
    scale = chan_ref[:, 3:4]
    g_ref[...] = g_sum * scale
    total = jnp.sum(g_sum * w_out_ref[...].astype(F32), axis=1, keepdims=True)
    sum_grad = sums[:, 52:53]
    lane = lane_iota((C, 128))
    sums = jnp.where(lane == 53, total + chan_ref[:, 4:5] * sum_grad, sums)
    sums = jnp.where(lane == 52, sum_grad * scale, sums)
    flat = jnp.transpose(sums)
    for p in range(TAPS):
        taps_ref[p] = flat[TAPS * p : TAPS * (p + 1)]
    vectors_ref[...] = flat[48:56]


def ring(axis, count):
    ahead = [(i, (i + 1) % count) for i in range(count)]
    return functools.partial(lax.ppermute, axis_name=axis, perm=ahead), functools.partial(
        lax.ppermute, axis_name=axis, perm=[(b, a) for a, b in ahead]
    )


def add_rims(head, tail, up, down):
    ahead, behind = ring("lon", lax.axis_size("lon"))
    rims = ahead(tail) + behind(head)
    up = jnp.concatenate([up[:, : PACK - 128], up[:, PACK - 128 :] + rims], axis=1)
    down = jnp.concatenate([down[:, : PACK - 128], down[:, PACK - 128 :] + rims], axis=1)
    return rims, up, down


def lat_rows(up, down):
    count = lax.axis_size("lat")
    above = lax.ppermute(down, "lat", [(i, i + 1) for i in range(count - 1)])
    below = lax.ppermute(up, "lat", [(i + 1, i) for i in range(count - 1)])
    return above, below


def swap(value, bits):
    count = lax.axis_size("lat") * lax.axis_size("lon")
    return lax.ppermute(value, ("lat", "lon"), [(i, i ^ bits) for i in range(count)])


def rounded(value):
    return lax.reduce_precision(value, 8, 7)


def by_index(index, parts):
    low = jnp.where((index & 1) != 0, parts[1], parts[0])
    high = jnp.where((index & 1) != 0, parts[3], parts[2])
    return jnp.where((index & 2) != 0, high, low)


def halved(value):
    core = lax.axis_index("lon") & 1
    half = value.shape[0] // 2
    low, high = value[:half], value[half:]
    sent = jnp.where(core != 0, low, high)
    return jnp.where(core != 0, high, low) + swap(sent, 1)


def all_sum(value, hooks):
    me = lax.axis_index("lat") * lax.axis_size("lon") + lax.axis_index("lon")
    core, z = me & 1, (me >> 2) & 3
    value = hooks(1, halved(hooks(0, value)))
    size = value.shape[0] // 4
    quarters = [value[size * k : size * (k + 1)] for k in range(4)]
    total = by_index(z, quarters)
    for k in range(1, 4):
        total = total + swap(by_index(z ^ k, quarters).astype(BF16), 4 * k).astype(F32)
    value = total
    step = 2
    for first, second in ((32, 64), (2, 16)):
        value = hooks(step, value)
        step += 1
        mine = rounded(value)
        sent = mine.astype(BF16)
        near, far, both = (swap(sent, b).astype(F32) for b in (first, second, first | second))
        value = (mine + near) + (far + both)
    value = hooks(4, rounded(value).astype(BF16))
    parts = [value] + [swap(value, 4 * k) for k in range(1, 4)]
    value = jnp.concatenate([by_index(z ^ k, parts) for k in range(4)], axis=0)
    value = hooks(5, value)
    other = swap(value, 1)
    width = value.shape[1] - 256
    taps = value[:, width:].astype(F32) + other[:, width:].astype(F32)
    taps = taps.reshape(4, C // 8, 2, 128)
    taps = jnp.transpose(taps, (0, 2, 1, 3)).reshape(C, 128)
    value, other = value[:, :width], other[:, :width]
    low, high = jnp.where(core != 0, other, value), jnp.where(core != 0, value, other)
    return jnp.concatenate([low, high], axis=0), taps


def local(
    stash_input, input_low, input_high, stash_hidden, hidden_low, hidden_high, grad_out,
    kernel, conv_bias, norm_gain, norm_bias, w_in, w_out, out_bias, layer_scale,
):
    tie = lax.optimization_barrier

    def shape(*dims, dtype=F32):
        return jax.ShapeDtypeStruct(dims, dtype)

    field_shape = shape(ROWS, C, LANES, dtype=BF16)
    total_shape = shape(ROWS, C, LANES)
    rim_shape = shape(C, 128, dtype=BF16)
    pack_shape = shape(C, PACK, dtype=BF16)
    sums_shape = shape(C, 128)
    weight_shape = shape(C, FF)
    own, head, tail, up, down = resident(
        restore_kernel,
        "restore",
        (field_shape, rim_shape, rim_shape, pack_shape, pack_shape),
        stash_input,
        input_low,
        input_high,
        scratch=[
            pltpu.VMEM(stash_input.shape, jnp.int32),
            pltpu.VMEM(input_low.shape, BF16),
            pltpu.VMEM(input_high.shape, BF16),
            pltpu.VMEM((2, C // GROUP, ROWS, LANES), F32),
            pltpu.SemaphoreType.DMA((3,)),
        ],
        space=pltpu.HBM,
    )
    rims, up, down = add_rims(head, tail, up, down)
    above, below = lat_rows(up, down)

    taps = jnp.pad(kernel.reshape(C, TAPS * TAPS), ((0, 0), (0, 128 - TAPS * TAPS)))
    chan = jnp.stack([conv_bias, norm_gain, norm_bias, layer_scale, out_bias], axis=1)
    chan = jnp.pad(chan, ((0, 0), (0, 123)))
    w_out_t = jnp.transpose(w_out)
    stencil_scratch = [
        pltpu.VMEM((TAPS * TAPS, CH, 128), F32),
        pltpu.VMEM((TAPS, ROWS, CH, LANES), F32),
    ]
    hidden_back, normed_back, g_part, sums_a, grad_rows = resident(
        mlp_kernel,
        "mlp",
        (
            shape(ROWS, FF, LANES, dtype=BF16),
            total_shape,
            weight_shape,
            sums_shape,
            field_shape,
        ),
        stash_hidden,
        hidden_low,
        hidden_high,
        grad_out,
        chan,
        w_out_t,
        w_in,
        space=pltpu.HBM,
        scratch=[
            pltpu.VMEM(stash_hidden.shape, jnp.int32),
            pltpu.VMEM(hidden_low.shape, BF16),
            pltpu.VMEM(hidden_high.shape, BF16),
            pltpu.VMEM(grad_out.shape, BF16),
            pltpu.VMEM(chan.shape, F32),
            pltpu.VMEM((C, FF), BF16),
            pltpu.VMEM((C, FF), BF16),
            pltpu.SemaphoreType.DMA((7,)),
            pltpu.VMEM((FF, FF), BF16),
            pltpu.VMEM((FF, C), BF16),
            pltpu.VMEM((C, FF), BF16),
            pltpu.VMEM((FF, LANES), F32),
            pltpu.VMEM((FF, LANES), BF16),
            pltpu.VMEM((8, FF // GROUP, ROWS, LANES), F32),
            pltpu.VMEM(grad_out.shape, F32),
        ],
    )

    def over_own(own, rims, flip, name):
        return resident(
            functools.partial(own_kernel, flip=flip),
            name,
            (field_shape, total_shape),
            own,
            rims,
            taps,
            scratch=stencil_scratch,
        )

    filled, total = over_own(own, rims, False, "conv_own")
    field, grad_own, head, tail, up, down, normed_in, sums_b = resident(
        conv_kernel,
        "conv",
        (
            shape(ROWS + 2 * RADIUS, C, LANES, dtype=BF16),
            field_shape,
            rim_shape,
            rim_shape,
            pack_shape,
            pack_shape,
            field_shape,
            sums_shape,
        ),
        filled,
        total,
        above,
        below,
        taps,
        chan,
        normed_back,
        scratch=[pltpu.VMEM((ROWS, C, LANES), F32), pltpu.VMEM((3, C, 128), F32)]
        + stencil_scratch,
    )

    h_part = resident(
        weight_kernel,
        "weight",
        weight_shape,
        normed_in,
        hidden_back,
        scratch=[pltpu.VMEM((FF, FF), BF16)],
    )
    rims, up, down = add_rims(head, tail, up, down)
    above, below = lat_rows(up, down)
    late = {"own": grad_own, "above": above, "below": below}

    def hooks(step, value):
        if step == 1:
            value, late["grad"], _ = tie((value, grad_own, up))
            late["taps"] = resident(taps_kernel, "taps", sums_shape, field, late["grad"])
            parts = late["taps"].reshape(4, 2, C // 8, 128)
            parts = [parts[:, k].reshape(C // 2, 128) for k in range(2)]
            value = jnp.concatenate([value, *parts], axis=1)
            value, late["own"] = tie((value, late["own"]))
            late["total"] = over_own(late["own"], rims, True, "input_own")[1]
        elif step == 3:
            above, below, late["total"] = tie((late["above"], late["below"], late["total"]))
            halo = resident(
                halo_kernel,
                "halo",
                shape(2 * RADIUS, C, LANES, dtype=BF16),
                above,
                below,
                cost=0,
            )
            value, late["total"], late["halo"] = tie((value, late["total"], halo))
        elif step == 4:
            value, late["total"] = tie((value, late["total"]))
            late["input"] = resident(
                input_kernel,
                "input",
                field_shape,
                late["total"],
                late["halo"],
                taps,
                grad_rows,
                scratch=stencil_scratch,
            )
        elif step == 5:
            value, late["input"] = tie((value, late["input"]))
            late["input"] = jnp.transpose(late["input"][:, :, :COLS], (1, 0, 2))
        return value

    summed, summed_taps = all_sum(jnp.concatenate([g_part, h_part, sums_a + sums_b], axis=1), hooks)
    cells = ROWS * lax.axis_size("lat") * COLS * lax.axis_size("lon")
    g_sum, h_sum, grad_kernel, vectors = resident(
        functools.partial(final_kernel, factor=1.0 / math.sqrt(cells)),
        "final",
        (weight_shape, weight_shape, shape(TAPS, TAPS, C), shape(8, C)),
        summed,
        summed_taps,
        chan,
        w_out_t,
    )
    return (
        late["input"],
        jnp.transpose(grad_kernel, (2, 0, 1)),
        vectors[3],
        vectors[1],
        vectors[2],
        h_sum,
        jnp.transpose(g_sum),
        vectors[4],
        vectors[5],
    )


def solution(mesh):
    split = P(None, "lat", "lon")
    return jax.shard_map(
        local,
        mesh=mesh,
        in_specs=(split,) * 7 + (P(),) * 8,
        out_specs=(split,) + (P(),) * 8,
        check_vma=False,
    )
```
